32 devices in a mesh: dp: 8 (over y, x, core), tensor: 4 (over z).
Axes of the slice: x: 2, y: 2, z: 4, core: 2. Of those that a mesh axis runs over, the one named last changes fastest.
Arguments:
- hidden_in: bfloat16 [32768, 768], P(('dp', 'tensor')), may hold values from -6 to 6
- seg_ids: int32 [32768], P('dp'), may hold values from 0 to 559, as said below
- norm1_gain: float32 [768], replicated, may hold values from 0.1 to 1.9
- norm2_gain: float32 [768], replicated, may hold values from 0.1 to 1.9
- qkv_weight: bfloat16 [768, 3, 12, 64], P(None, None, 'tensor'), may hold values from -0.21875 to 0.21875
- attn_weight: bfloat16 [768, 768], P('tensor'), may hold values from -0.875 to 0.875
- mlp_in_weight: bfloat16 [768, 2, 1152], P(None, None, 'tensor'), may hold values from -0.21875 to 0.21875
- mlp_out_weight: bfloat16 [1152, 768], P('tensor'), may hold values from -0.1875 to 0.1875
- out_grad: bfloat16 [32768, 768], P(('dp', 'tensor')), may hold values from -6 to 6
Outputs:
- layer_out: bfloat16 [32768, 768], P(('dp', 'tensor'))
- grad_hidden: bfloat16 [32768, 768], P(('dp', 'tensor'))
- grad_norm1_gain: float32 [768], replicated
- grad_norm2_gain: float32 [768], replicated
- grad_qkv_weight: float32 [768, 3, 12, 64], P(None, None, 'tensor')
- grad_attn_weight: float32 [768, 768], P('tensor')
- grad_mlp_in_weight: float32 [768, 2, 1152], P(None, None, 'tensor')
- grad_mlp_out_weight: float32 [1152, 768], P('tensor')
The draws below stay inside these ranges and needn't reach their ends.
Inputs may be any that keep to these rules, and one draw needn't show every extreme that they name: `seg_ids`: within each sequence of 2048 tokens the id rises by exactly one from each document to the next; no id is shared by two sequences; a document has 1 to 800 tokens and every sequence holds one document of exactly 800 tokens.
All inputs are finite; a program needn't handle non-finite values.
Results may differ from the reference program's by a relative error of at most 0.02.
Values may be sent and summed in bfloat16 or wider, within the bound.
No kernel may reach another device: no remote copies, remote signals or barrier semaphores. Data moves between devices by JAX's collectives and lax.ppermute only.
A program may use at most 192 MiB of HBM per device.

```python
import jax
import jax.numpy as jnp
from jax import lax

D = 768
HEADS = 12
HEAD_DIM = 64
FF = 1152
WINDOW = 128
SEQ_LEN = 2048
DOC_MIN = 60
DOC_MAX = 800
TOKENS = 32768


def draw_seg_ids(key, part):
    key = jax.random.fold_in(key, 11)
    seq_count = TOKENS // SEQ_LEN
    most_docs = SEQ_LEN // DOC_MIN + 1
    len_key, pick_key = jax.random.split(key)
    lengths = jax.random.randint(len_key, (seq_count, most_docs), DOC_MIN, DOC_MAX + 1)
    chosen = jax.random.randint(pick_key, (seq_count, 1), 0, 2)
    slot_idx = jnp.arange(most_docs, dtype=jnp.int32)[None, :]
    lengths = jnp.where(slot_idx == chosen, DOC_MAX, lengths).astype(jnp.int32)
    doc_ends = jnp.cumsum(lengths, axis=1)
    places = jnp.arange(SEQ_LEN, dtype=jnp.int32)[None, :, None]
    local_doc = jnp.sum((doc_ends[:, None, :] <= places).astype(jnp.int32), axis=2)
    last_doc = local_doc[:, -1:]
    final_row = (jnp.arange(seq_count, dtype=jnp.int32) == seq_count - 1)[:, None]
    shift_vals = jnp.where(final_row, most_docs - 1 - last_doc, 0).astype(jnp.int32)
    seq_base = (jnp.arange(seq_count, dtype=jnp.int32) * most_docs)[:, None]
    return (local_doc + seq_base + shift_vals).reshape(-1).astype(jnp.int32)


def block_scale(stream_key, extent, cuts, low, largest):
    def one(dim, blocks):
        draws = jax.random.uniform(jax.random.fold_in(jax.random.fold_in(stream_key, 6), dim), (blocks,), jnp.float32, low / len(cuts), largest / len(cuts))
        return jnp.repeat(jnp.exp(draws), extent[dim] // blocks).reshape((-1,) + (1,) * (len(extent) - dim - 1))

    factor_of = one(*cuts[0])
    for cut in cuts[1:]:
        factor_of = factor_of * one(*cut)
    return factor_of


def bell_draw(own_key, extent, deviation, bound, cuts=(), held_as=jnp.bfloat16):
    entries = deviation * jax.random.normal(own_key, extent, jnp.float32)
    if cuts:
        entries = entries * block_scale(own_key, extent, cuts, -0.22, 0.18)
    return jnp.clip(entries, -bound, bound).astype(held_as)


def setup_inputs(seed: int = 0) -> dict:
    arg_keys = jax.random.split(jax.random.key(seed), 10)
    hidden_in = bell_draw(arg_keys[0], (TOKENS, D), 1.0, 6.0, ((0, 32),))
    seg_ids = draw_seg_ids(jax.random.fold_in(arg_keys[9], 71), 0)
    norm1_gain = jnp.clip(1.0 + 0.18 * jax.random.normal(arg_keys[2], (D,), jnp.float32), 0.1, 1.9)
    norm2_gain = jnp.clip(1.0 + 0.18 * jax.random.normal(arg_keys[3], (D,), jnp.float32), 0.1, 1.9)
    qkv_weight = bell_draw(arg_keys[4], (D, 3, HEADS, HEAD_DIM), D ** -0.5, 0.21875, ((2, 4),))
    attn_weight = bell_draw(arg_keys[5], (D, D), (D // 16) ** -0.5, 0.875, ((0, 4),))
    mlp_in_weight = bell_draw(arg_keys[6], (D, 2, FF), D ** -0.5, 0.21875, ((2, 4),))
    mlp_out_weight = bell_draw(arg_keys[7], (FF, D), FF ** -0.5, 0.1875, ((0, 4),))
    out_grad = bell_draw(arg_keys[8], (TOKENS, D), 1.0, 6.0, ((0, 32),))
    return {"hidden_in": hidden_in, "seg_ids": seg_ids, "norm1_gain": norm1_gain, "norm2_gain": norm2_gain, "qkv_weight": qkv_weight, "attn_weight": attn_weight, "mlp_in_weight": mlp_in_weight, "mlp_out_weight": mlp_out_weight, "out_grad": out_grad}


eps_norm = 1e-05
rope_base = 10000.0
highest = lax.Precision.HIGHEST

@jax.custom_vjp
def low(v):
    return lax.optimization_barrier(v.astype(jnp.bfloat16)).astype(jnp.float32)

@jax.custom_vjp
def low_back(v):
    return v

def low_keep(v):
    return (low(v), None)

def low_pass(kept, grad):
    return (grad,)

def back_keep(v):
    return (v, None)

def back_low(kept, grad):
    return (low(grad),)
low.defvjp(low_keep, low_pass)
low_back.defvjp(back_keep, back_low)

def layer_norm(row_vals, gain_vec):
    average = lax.optimization_barrier(jnp.mean(row_vals, axis=-1, keepdims=True))
    centered = row_vals - average
    spread_sq = lax.optimization_barrier(jnp.mean(centered * centered, axis=-1, keepdims=True))
    return centered * lax.rsqrt(spread_sq + eps_norm) * gain_vec

def doc_positions(seg_ids):
    count_all = seg_ids.shape[0]
    places = jnp.arange(count_all, dtype=jnp.int32)
    earlier = jnp.concatenate([jnp.full((1,), -1, jnp.int32), seg_ids[:-1]])
    starts = jnp.where(seg_ids != earlier, places, 0).astype(jnp.int32)
    return places - lax.cummax(starts, axis=0)

def rope_tables(positions, head_dim):
    freq_vals = rope_base ** (-jnp.arange(0, head_dim, 2).astype(jnp.float32) / head_dim)
    angles = positions.astype(jnp.float32)[:, None] * freq_vals[None, :]
    angles = jnp.concatenate([angles, angles], axis=1)
    return (jnp.cos(angles), jnp.sin(angles))

def rotate(arr_vals, cosine_tab, sine_tab):
    width_half = arr_vals.shape[-1] // 2
    turned = jnp.concatenate([-arr_vals[..., width_half:], arr_vals[..., :width_half]], axis=-1)
    return arr_vals * cosine_tab[:, None, :] + turned * sine_tab[:, None, :]

def window_attention(queries, key_vals, value_vals, seg_part):
    window_half = WINDOW // 2
    seq_rows = queries.shape[0]
    block_rows = min(512, seq_rows)
    key_rows = block_rows + 2 * window_half
    keys_ext = jnp.pad(key_vals, ((window_half, window_half), (0, 0), (0, 0)))
    values_ext = jnp.pad(value_vals, ((window_half, window_half), (0, 0), (0, 0)))
    seg_key = jnp.pad(seg_part, (window_half, window_half), constant_values=-1)
    scale_factor = queries.shape[-1] ** (-0.5)

    @jax.checkpoint
    def one_block(block_idx):
        first_row = block_idx * block_rows
        q_blk = lax.dynamic_slice_in_dim(queries, first_row, block_rows, 0)
        k_blk = lax.dynamic_slice_in_dim(keys_ext, first_row, key_rows, 0)
        v_blk = lax.dynamic_slice_in_dim(values_ext, first_row, key_rows, 0)
        seg_q = lax.dynamic_slice_in_dim(seg_part, first_row, block_rows, 0)
        seg_k = lax.dynamic_slice_in_dim(seg_key, first_row, key_rows, 0)
        q_place = jnp.arange(block_rows, dtype=jnp.int32)[:, None]
        k_place = jnp.arange(key_rows, dtype=jnp.int32)[None, :] - window_half
        allowed = (jnp.abs(q_place - k_place) <= window_half) & (seg_q[:, None] == seg_k[None, :])
        scores = low_back(scale_factor * jnp.einsum('qhe,khe->hqk', q_blk, k_blk, precision=highest))
        scores = jnp.where(allowed[None], scores, -1e+30)
        prob_vals = jax.nn.softmax(scores, axis=-1)
        return jnp.einsum('hqk,khe->qhe', low(prob_vals), v_blk, precision=highest)
    blk_out = lax.map(one_block, jnp.arange(seq_rows // block_rows))
    return blk_out.reshape(queries.shape)

def layer(resid, norm1_gain, norm2_gain, qkv_weight, attn_weight, mlp_in_weight, mlp_out_weight, seg_part, pos_part):
    seq_rows, model_width = resid.shape
    head_count = qkv_weight.shape[2]
    head_dim = qkv_weight.shape[3]
    low_one = low(layer_norm(resid, norm1_gain))
    mixed_rows = low_back(jnp.dot(low_one, qkv_weight.reshape(model_width, -1), precision=highest))
    mixed_rows = mixed_rows.reshape(seq_rows, 3, head_count, head_dim)
    cosine_tab, sine_tab = rope_tables(pos_part, head_dim)
    queries = low(rotate(mixed_rows[:, 0], cosine_tab, sine_tab))
    key_vals = low(rotate(mixed_rows[:, 1], cosine_tab, sine_tab))
    value_vals = low(mixed_rows[:, 2])
    attn_vals = window_attention(queries, key_vals, value_vals, seg_part)
    low_attn = low(low_back(attn_vals.reshape(seq_rows, model_width)))
    middle = resid + low_back(jnp.dot(low_attn, attn_weight, precision=highest))
    low_two = low(layer_norm(middle, norm2_gain))
    gate_up = low_back(jnp.dot(low_two, mlp_in_weight.reshape(model_width, -1), precision=highest))
    ff_width = mlp_in_weight.shape[2]
    act_vals = jax.nn.gelu(gate_up[:, :ff_width], approximate=False) * gate_up[:, ff_width:]
    low_act = low(act_vals)
    return middle + low_back(jnp.dot(low_act, mlp_out_weight, precision=highest))

def reference(hidden_in, seg_ids, norm1_gain, norm2_gain, qkv_weight, attn_weight, mlp_in_weight, mlp_out_weight, out_grad):
    positions = doc_positions(seg_ids)
    params = tuple((weight_arr.astype(jnp.float32) for weight_arr in (norm1_gain, norm2_gain, qkv_weight, attn_weight, mlp_in_weight, mlp_out_weight)))
    seq_count = hidden_in.shape[0] // SEQ_LEN
    model_width = hidden_in.shape[1]
    resid_all = hidden_in.astype(jnp.float32).reshape(seq_count, SEQ_LEN, model_width)
    grad_all = out_grad.astype(jnp.float32).reshape(seq_count, SEQ_LEN, model_width)
    seg_all = seg_ids.reshape(seq_count, SEQ_LEN)
    pos_all = positions.reshape(seq_count, SEQ_LEN)

    def seq_step(totals, pieces):
        resid, seg_part, pos_part, grad_part = pieces

        def forward(resid_arg, gain_one, gain_two, w_qkv, w_attn, w_in, w_out):
            return layer(resid_arg, gain_one, gain_two, w_qkv, w_attn, w_in, w_out, seg_part, pos_part)
        output, pullback = jax.vjp(forward, resid, *params)
        grads = pullback(grad_part)
        new_totals = tuple((left_sum + right_sum for left_sum, right_sum in zip(totals, grads[1:])))
        return (new_totals, (output.astype(jnp.bfloat16), grads[0].astype(jnp.bfloat16)))
    zero_totals = tuple((jnp.zeros_like(weight_arr) for weight_arr in params))
    totals, (outputs, grad_rows) = lax.scan(seq_step, zero_totals, (resid_all, seg_all, pos_all, grad_all))
    layer_out = outputs.reshape(hidden_in.shape)
    grad_hidden = grad_rows.reshape(hidden_in.shape)
    return (layer_out, grad_hidden, totals[0], totals[1], totals[2], totals[3], totals[4], totals[5])
```

```python
import jax
import jax.numpy as jnp
from jax import lax
from jax.experimental import pallas as pl
from jax.experimental.pallas import tpu as pltpu
from jax.sharding import PartitionSpec as P

WINDOW = 128
HALF = WINDOW // 2
EPS = 1e-05
ROPE_BASE = 10000.0
BLK = 128
CORE, XBIT, YBIT = 1, 2, 4
bf16 = jnp.bfloat16
f32 = jnp.float32
MIB = 1024 * 1024


def nn(a, b):
    return lax.dot_general(a, b, (((1,), (0,)), ((), ())), preferred_element_type=f32)


def nt(a, b):
    return lax.dot_general(a, b, (((1,), (1,)), ((), ())), preferred_element_type=f32)


def tn(a, b):
    return lax.dot_general(a, b, (((0,), (0,)), ((), ())), preferred_element_type=f32)


def row_stats(x):
    mean = jnp.mean(x, axis=-1, keepdims=True)
    cen = x - mean
    inv = lax.rsqrt(jnp.mean(cen * cen, axis=-1, keepdims=True) + EPS)
    return cen * inv, inv


def fold_rows(x):
    return jnp.sum(x.reshape(x.shape[0] // 8, 8, x.shape[1]), axis=0)


def const_spec(shape):
    zeros = (0,) * len(shape)
    return pl.BlockSpec(shape, lambda i: zeros, pipeline_mode=pl.Buffered(1))


def row_spec(rows, cols):
    return pl.BlockSpec((rows, cols), lambda i: (i, 0))


def params(mib):
    return pltpu.CompilerParams(
        dimension_semantics=("arbitrary",), vmem_limit_bytes=mib * MIB
    )


def turn_lanes(z, lo_sign):
    width = z.shape[1]
    lane = lax.broadcasted_iota(jnp.int32, (1, width), 1)
    first = lane % 64 < 32
    ahead = pltpu.roll(z, width - 32, 1)
    behind = pltpu.roll(z, 32, 1)
    return jnp.where(first, lo_sign * ahead, -lo_sign * behind)


def qkv_kernel(x_ref, gain_ref, w_ref, cos_ref, sin_ref, low_ref, q_ref, k_ref, v_ref):
    normed, _ = row_stats(x_ref[...].astype(f32))
    low = (normed * gain_ref[...]).astype(bf16)
    low_ref[...] = low
    width = low.shape[1]
    cos = jnp.concatenate([cos_ref[...]] * (width // 128), axis=1)
    sin = jnp.concatenate([sin_ref[...]] * (width // 128), axis=1)
    q = nt(low, w_ref[0])
    q_ref[...] = (q * cos + turn_lanes(q, -1.0) * sin).astype(bf16)
    k = nt(low, w_ref[1])
    k_ref[...] = (k * cos + turn_lanes(k, -1.0) * sin).astype(bf16)
    v_ref[...] = nt(low, w_ref[2]).astype(bf16)


def qkv_call(x_ext, gain, w, cos, sin):
    rows, width = x_ext.shape
    blk = rows // 3
    out = jax.ShapeDtypeStruct((rows, width), bf16)
    return pl.pallas_call(
        qkv_kernel,
        grid=(rows // blk,),
        in_specs=[
            row_spec(blk, width),
            const_spec((1, width)),
            const_spec(w.shape),
            row_spec(blk, 128),
            row_spec(blk, 128),
        ],
        out_specs=[row_spec(blk, width)] * 4,
        out_shape=[out] * 4,
        compiler_params=params(40),
        cost_estimate=pl.CostEstimate(
            flops=6 * rows * width * width, bytes_accessed=14 * MIB, transcendentals=0
        ),
        name="qkv",
    )(x_ext, gain, w, cos, sin)


def stack_pair(z, scale):
    lane = lax.broadcasted_iota(jnp.int32, (1, 128), 1)
    low_head = (lane < 64).astype(f32) * scale
    high_head = (lane >= 64).astype(f32) * scale
    return jnp.concatenate([z * low_head.astype(bf16), z * high_head.astype(bf16)], axis=0)


def merge_pair(z):
    rows = z.shape[0] // 2
    lane = lax.broadcasted_iota(jnp.int32, (1, 128), 1)
    return jnp.where(lane < 64, z[:rows], z[rows:])


def attend_kernel(q_ref, k_ref, v_ref, bias_ref, out_ref, lse_ref):
    b = pl.program_id(0)
    start = pl.multiple_of(b * BLK, BLK)
    bias = bias_ref[0]
    bias = jnp.concatenate([bias, bias], axis=1)
    for j in range(q_ref.shape[1] // 128):
        cols = slice(128 * j, 128 * j + 128)
        qs = stack_pair(q_ref[pl.ds(start + HALF, BLK), cols], 0.125)
        kb = k_ref[pl.ds(start, 2 * BLK), cols]
        vb = v_ref[pl.ds(start, 2 * BLK), cols]
        s = nt(kb, qs) + bias
        top = jnp.max(s, axis=0, keepdims=True)
        e = jnp.exp(s - top)
        total = jnp.sum(e, axis=0, keepdims=True)
        low_p = (e * (1.0 / total)).astype(bf16)
        out_ref[:, cols] = merge_pair(tn(low_p, vb)).astype(bf16)
        lse_ref[0, j : j + 1, :] = top + jnp.log(total)


def attend_call(q, k, v, bias, rows):
    ext, width = q.shape
    blocks = rows // BLK
    return pl.pallas_call(
        attend_kernel,
        grid=(blocks,),
        in_specs=[
            const_spec((ext, width)),
            const_spec((ext, width)),
            const_spec((ext, width)),
            pl.BlockSpec((1, 2 * BLK, BLK), lambda i: (i, 0, 0)),
        ],
        out_specs=[row_spec(BLK, width), pl.BlockSpec((1, 8, 2 * BLK), lambda i: (i, 0, 0))],
        out_shape=[
            jax.ShapeDtypeStruct((rows, width), bf16),
            jax.ShapeDtypeStruct((blocks, 8, 2 * BLK), f32),
        ],
        compiler_params=params(32),
        cost_estimate=pl.CostEstimate(
            flops=12 * rows * 256 * width, bytes_accessed=9 * MIB, transcendentals=rows * 3072
        ),
        name="attend",
    )(q, k, v, bias)


def mlp_kernel(
    x_ref,
    og_ref,
    attn_ref,
    gain_ref,
    wa_ref,
    wi_ref,
    wo_ref,
    out_ref,
    gmid_ref,
    lowmid_ref,
    dattn_ref,
    low2_ref,
    act_ref,
    ggu_ref,
    gain_grad_ref,
):
    gain = gain_ref[...]
    middle = x_ref[...].astype(f32) + nn(attn_ref[...], wa_ref[...])
    normed, inv = row_stats(middle)
    low_two = (normed * gain).astype(bf16)
    low2_ref[...] = low_two
    og = og_ref[...]
    ff = wo_ref.shape[0]
    chunk = 384
    result = middle
    grad_n = jnp.zeros(middle.shape, f32)
    for c in range(ff // chunk):
        sl = slice(c * chunk, c * chunk + chunk)
        gate = nt(low_two, wi_ref[0, sl])
        up = nt(low_two, wi_ref[1, sl])
        wo = wo_ref[sl]
        phi = 0.5 + 0.5 * lax.erf(gate * (0.5**0.5))
        gel = gate * phi
        act = (gel * up).astype(bf16)
        act_ref[:, sl] = act
        result = result + nn(act, wo)
        grad_act = nt(og, wo)
        dens = jnp.exp(-0.5 * gate * gate) * 0.3989422804014327
        g_gate = (grad_act * up * (phi + gate * dens)).astype(bf16)
        g_up = (grad_act * gel).astype(bf16)
        ggu_ref[:, sl] = g_gate
        ggu_ref[:, ff + c * chunk : ff + c * chunk + chunk] = g_up
        grad_n = grad_n + nn(g_gate, wi_ref[0, sl]) + nn(g_up, wi_ref[1, sl])
    out_ref[...] = result.astype(bf16)

    @pl.when(pl.program_id(0) == 0)
    def _():
        gain_grad_ref[...] = jnp.zeros(gain_grad_ref.shape, f32)

    gain_grad_ref[...] += fold_rows(grad_n * normed)
    u = grad_n * gain
    grad_mid = og.astype(f32) + inv * (
        u
        - jnp.mean(u, axis=-1, keepdims=True)
        - normed * jnp.mean(u * normed, axis=-1, keepdims=True)
    )
    gmid_ref[...] = grad_mid
    low_mid = grad_mid.astype(bf16)
    lowmid_ref[...] = low_mid
    dattn_ref[...] = nt(low_mid, wa_ref[...]).astype(bf16)


def mlp_call(x, og, attn, gain, wa, wi, wo):
    rows, width = x.shape
    ff = wo.shape[0]
    blk = 256
    low = jax.ShapeDtypeStruct((rows, width), bf16)
    return pl.pallas_call(
        mlp_kernel,
        grid=(rows // blk,),
        in_specs=[row_spec(blk, width)] * 3
        + [const_spec((1, width)), const_spec(wa.shape), const_spec(wi.shape), const_spec(wo.shape)],
        out_specs=[row_spec(blk, width)] * 5
        + [row_spec(blk, ff), row_spec(blk, 2 * ff), pl.BlockSpec((8, width), lambda i: (0, 0))],
        out_shape=[
            low,
            jax.ShapeDtypeStruct((rows, width), f32),
            low,
            low,
            low,
            jax.ShapeDtypeStruct((rows, ff), bf16),
            jax.ShapeDtypeStruct((rows, 2 * ff), bf16),
            jax.ShapeDtypeStruct((8, width), f32),
        ],
        compiler_params=params(48),
        cost_estimate=pl.CostEstimate(
            flops=4 * rows * width * (width + 3 * ff),
            bytes_accessed=30 * MIB,
            transcendentals=2 * rows * ff,
        ),
        name="mlp",
    )(x, og, attn, gain, wa, wi, wo)


def attend_back_kernel(
    q_ref,
    k_ref,
    v_ref,
    do_ref,
    bias_ref,
    lse_ref,
    cos_ref,
    sin_ref,
    dq_ref,
    dk_ref,
    dv_ref,
    edge_ref,
):
    b = pl.program_id(0)
    start = pl.multiple_of(b * BLK, BLK)

    @pl.when(b == 0)
    def _():
        dk_ref[...] = jnp.zeros(dk_ref.shape, f32)
        dv_ref[...] = jnp.zeros(dv_ref.shape, f32)

    bias = bias_ref[0]
    bias = jnp.concatenate([bias, bias], axis=1)
    rows = pl.ds(start, 2 * BLK)
    cos = cos_ref[pl.ds(start + HALF, BLK), :] * 0.125
    sin = sin_ref[pl.ds(start + HALF, BLK), :] * 0.125
    for j in range(q_ref.shape[1] // 128):
        cols = slice(128 * j, 128 * j + 128)
        qs = stack_pair(q_ref[pl.ds(start + HALF, BLK), cols], 0.125)
        dos = stack_pair(do_ref[:, cols], 1.0)
        kb = k_ref[rows, cols]
        vb = v_ref[rows, cols]
        p = jnp.exp(nt(kb, qs) + bias - lse_ref[0, j : j + 1, :])
        dp = nt(vb, dos)
        dot = jnp.sum(p * dp, axis=0, keepdims=True)
        ds = (p * (dp - dot)).astype(bf16)
        dv_ref[rows, cols] += nn(p.astype(bf16), dos)
        dk_ref[rows, cols] += nn(ds, qs)
        dq = merge_pair(tn(ds, kb))
        dq_ref[:, cols] = (dq * cos + turn_lanes(dq * sin, 1.0)).astype(bf16)

    @pl.when(b == pl.num_programs(0) - 1)
    def _():
        width = dk_ref.shape[1]
        ext = dk_ref.shape[0]
        for at, ref in ((0, dk_ref), (width, dv_ref)):
            edge_ref[:HALF, at : at + width] = ref[:HALF, :].astype(bf16)
            edge_ref[HALF:, at : at + width] = ref[ext - HALF :, :].astype(bf16)


def attend_back_call(q, k, v, do, bias, lse, cos, sin):
    ext, width = q.shape
    rows = do.shape[0]
    full = const_spec((ext, width))
    acc = pl.BlockSpec((ext, width), lambda i: (0, 0))
    return pl.pallas_call(
        attend_back_kernel,
        grid=(rows // BLK,),
        in_specs=[
            full,
            full,
            full,
            row_spec(BLK, width),
            pl.BlockSpec((1, 2 * BLK, BLK), lambda i: (i, 0, 0)),
            pl.BlockSpec((1, 8, 2 * BLK), lambda i: (i, 0, 0)),
            const_spec((ext, 128)),
            const_spec((ext, 128)),
        ],
        out_specs=[
            row_spec(BLK, width),
            acc,
            acc,
            pl.BlockSpec((WINDOW, 2 * width), lambda i: (0, 0)),
        ],
        out_shape=[
            jax.ShapeDtypeStruct((rows, width), bf16),
            jax.ShapeDtypeStruct((ext, width), f32),
            jax.ShapeDtypeStruct((ext, width), f32),
            jax.ShapeDtypeStruct((WINDOW, 2 * width), bf16),
        ],
        compiler_params=params(48),
        cost_estimate=pl.CostEstimate(
            flops=30 * rows * 256 * width, bytes_accessed=20 * MIB, transcendentals=rows * 3072
        ),
        name="attend_back",
    )(q, k, v, do, bias, lse, cos, sin)


def mixed_kernel(dq_ref, dk_ref, dv_ref, first_ref, last_ref, cos_ref, sin_ref, mix_ref):
    width = dq_ref.shape[1]
    i = pl.program_id(0)
    mix_ref[:, :width] = dq_ref[...]
    cos = jnp.concatenate([cos_ref[...]] * (width // 128), axis=1)
    sin = jnp.concatenate([sin_ref[...]] * (width // 128), axis=1)
    pad = jnp.zeros((dk_ref.shape[0] - HALF, width), f32)
    is_first = (i == 0).astype(f32)
    is_last = (i == pl.num_programs(0) - 1).astype(f32)

    def joined(ref, at):
        cols = slice(at, at + width)
        head = first_ref[:, cols].astype(f32) * is_first
        tail = last_ref[:, cols].astype(f32) * is_last
        return ref[...] + jnp.concatenate([head, pad], axis=0) + jnp.concatenate([pad, tail], axis=0)

    dk = joined(dk_ref, 0)
    dv = joined(dv_ref, width)
    mix_ref[:, width : 2 * width] = (dk * cos + turn_lanes(dk * sin, 1.0)).astype(bf16)
    mix_ref[:, 2 * width :] = dv.astype(bf16)


def mixed_call(dq, dk, dv, first, last, cos, sin):
    rows, width = dq.shape
    blk = 256
    return pl.pallas_call(
        mixed_kernel,
        grid=(rows // blk,),
        in_specs=[row_spec(blk, width)] * 3
        + [const_spec(first.shape), const_spec(last.shape)]
        + [row_spec(blk, 128)] * 2,
        out_specs=row_spec(blk, 3 * width),
        out_shape=jax.ShapeDtypeStruct((rows, 3 * width), bf16),
        compiler_params=params(32),
        cost_estimate=pl.CostEstimate(
            flops=10 * rows * width, bytes_accessed=14 * MIB, transcendentals=0
        ),
        name="mixed",
    )(dq, dk, dv, first, last, cos, sin)


def input_grad_kernel(mix_ref, w_ref, x_ref, gmid_ref, gain_ref, out_ref, gain_grad_ref):
    grad_n = nn(mix_ref[...], w_ref[...])
    normed, inv = row_stats(x_ref[...].astype(f32))

    @pl.when(pl.program_id(0) == 0)
    def _():
        gain_grad_ref[...] = jnp.zeros(gain_grad_ref.shape, f32)

    gain_grad_ref[...] += fold_rows(grad_n * normed)
    u = grad_n * gain_ref[...]
    out_ref[...] = (
        gmid_ref[...]
        + inv
        * (
            u
            - jnp.mean(u, axis=-1, keepdims=True)
            - normed * jnp.mean(u * normed, axis=-1, keepdims=True)
        )
    ).astype(bf16)


def input_grad_call(mix, w, x, gmid, gain):
    rows, width = x.shape
    blk = 256
    return pl.pallas_call(
        input_grad_kernel,
        grid=(rows // blk,),
        in_specs=[
            row_spec(blk, 3 * width),
            const_spec(w.shape),
            row_spec(blk, width),
            row_spec(blk, width),
            const_spec((1, width)),
        ],
        out_specs=[row_spec(blk, width), pl.BlockSpec((8, width), lambda i: (0, 0))],
        out_shape=[
            jax.ShapeDtypeStruct((rows, width), bf16),
            jax.ShapeDtypeStruct((8, width), f32),
        ],
        compiler_params=params(40),
        cost_estimate=pl.CostEstimate(
            flops=6 * rows * width * width, bytes_accessed=16 * MIB, transcendentals=0
        ),
        name="input_grad",
    )(mix, w, x, gmid, gain)


def dp_swap(x, mask):
    count = lax.axis_size("dp")
    return lax.ppermute(x, "dp", [(i, i ^ mask) for i in range(count)])


def ring_shift(x, step):
    count = lax.axis_size("tensor")
    return lax.ppermute(x, "tensor", [(i, (i + step) % count) for i in range(count)])


def pair_swap(x):
    count = lax.axis_size("tensor")
    return lax.ppermute(x, "tensor", [(i, i ^ 1) for i in range(count)])


def index_dim(x, at, dim):
    return lax.squeeze(lax.dynamic_slice_in_dim(x, at, 1, dim), (dim,))


def core_rows(x, core, dim):
    rows = x.shape[dim]
    size = (rows // 2 + 7) // 8 * 8
    step = (rows - size) // 8
    tiles = x.reshape(x.shape[:dim] + (rows // 8, 8) + x.shape[dim + 1 :])
    part = lax.dynamic_slice_in_dim(tiles, core * step, size // 8, dim)
    return part.reshape(x.shape[:dim] + (size,) + x.shape[dim + 1 :])


def join_cores(a, b, rows, dim):
    size = a.shape[dim]
    keep = rows - size
    return jnp.concatenate([a, lax.slice_in_dim(b, size - keep, size, axis=dim)], axis=dim)


def spread_quads(piece):
    rows = piece.shape[1]
    half = (rows // 2 + 7) // 8 * 8
    from_x = dp_swap(piece, XBIT)
    from_y = dp_swap(piece, YBIT)
    diag = jnp.concatenate(
        [dp_swap(from_y[:, :half], XBIT), dp_swap(from_x[:, half:], YBIT)], axis=1
    )
    mine = [piece, from_x, from_y, diag]
    return mine, [dp_swap(part, CORE) for part in mine]


def gather_pieces(piece):
    steps = lax.axis_size("tensor")
    ring = jnp.stack([ring_shift(piece, s) for s in range(1, steps)])
    return spread_quads(ring)


def by_core(mine, theirs, core):
    first = core == 0
    return jnp.where(first, mine, theirs), jnp.where(first, theirs, mine)


def reduce_pieces(send, keep, quad):
    steps = keep.shape[0]
    half = steps // 2

    def add(a, b):
        return (a.astype(f32) + b.astype(f32)).astype(bf16)

    total = add(keep, dp_swap(send, CORE))
    rows, width = total.shape[2:]
    grid = total.reshape(steps, 2, 2, rows, width)
    x_at, y_at = quad & 1, quad >> 1
    first, second = grid[:half], grid[half:]

    def halve(arr, at, mask, dim):
        got = dp_swap(index_dim(arr, 1 - at, dim), mask)
        return add(index_dim(arr, at, dim), got)

    first = halve(first, x_at, XBIT, 2)
    second = halve(second, y_at, YBIT, 1)
    first = halve(first, y_at, YBIT, 1)
    second = halve(second, x_at, XBIT, 1)
    parts = [first[s] for s in range(half)] + [second[s] for s in range(steps - half)]
    mask = 8
    if lax.axis_size("dp") > mask:
        block = jnp.stack(parts)
        while mask < lax.axis_size("dp"):
            block = add(block, dp_swap(block, mask))
            mask *= 2
        parts = [block[s] for s in range(steps)]
    result = parts[0].astype(f32)
    for s in range(1, steps):
        result = result + ring_shift(parts[s], -s).astype(f32)
    return result.astype(bf16)


def put(buf, part, starts):
    return lax.dynamic_update_slice(buf, part, starts)


def tables(seg_ids, first_row, rows):
    count = seg_ids.shape[0]
    places = jnp.arange(count, dtype=jnp.int32)
    earlier = jnp.concatenate([jnp.full((1,), -1, jnp.int32), seg_ids[:-1]])
    starts = jnp.where(seg_ids != earlier, places, 0)
    positions = places - lax.cummax(starts, axis=0)
    ext = rows + WINDOW
    seg_ext = lax.dynamic_slice(jnp.pad(seg_ids, HALF, constant_values=-1), (first_row,), (ext,))
    pos_ext = lax.dynamic_slice(jnp.pad(positions, HALF), (first_row,), (ext,))
    freq = ROPE_BASE ** (-jnp.arange(0, 64, 2).astype(f32) / 64)
    angles = pos_ext.astype(f32)[:, None] * jnp.concatenate([freq] * 4)[None, :]
    blocks = rows // BLK
    seg_rows = seg_ext.reshape(blocks + 1, BLK)
    seg_k = jnp.concatenate([seg_rows[:-1], seg_rows[1:]], axis=1)
    seg_q = seg_ext[HALF : HALF + rows].reshape(blocks, BLK)
    k_place = jnp.arange(2 * BLK, dtype=jnp.int32)[:, None] - HALF
    q_place = jnp.arange(BLK, dtype=jnp.int32)[None, :]
    near = jnp.abs(k_place - q_place) <= HALF
    allowed = near[None] & (seg_k[:, :, None] == seg_q[:, None, :])
    bias = jnp.where(allowed, 0.0, -1e30).astype(f32)
    return jnp.cos(angles), jnp.sin(angles), bias


def body(
    hidden_in,
    seg_ids,
    norm1_gain,
    norm2_gain,
    qkv_weight,
    attn_weight,
    mlp_in_weight,
    mlp_out_weight,
    out_grad,
):
    rows, width = hidden_in.shape
    steps = lax.axis_size("tensor")
    here = lax.axis_index("tensor")
    at_dp = lax.axis_index("dp")
    core = at_dp & 1
    quad = (at_dp >> 1) & 3
    odd = (here & 1) == 1
    w_qkv = qkv_weight.transpose(1, 2, 3, 0).reshape(3, 4, 48, width)
    w_in = mlp_in_weight.transpose(1, 2, 0).reshape(2, 4, 72, width)
    w_out = mlp_out_weight.reshape(4, 72, width)
    w_attn = attn_weight.reshape(4, 48, width)

    edge = jnp.where(odd, hidden_in[:HALF], hidden_in[-HALF:])
    halo = pair_swap(edge)
    none = jnp.zeros_like(halo)
    x_ext = jnp.concatenate(
        [jnp.where(odd, halo, none), hidden_in, jnp.where(odd, none, halo)], axis=0
    )

    own_qkv = core_rows(index_dim(w_qkv, quad, 1), core, 1).reshape(3 * 24, width)
    mine, theirs = gather_pieces(own_qkv)
    qkv_all = jnp.zeros((3, steps, 4, 48, width), bf16)
    qkv_all = qkv_all.at[:, 0].set(w_qkv)
    for n in range(4):
        a, b = by_core(mine[n], theirs[n], core)
        a = a.reshape(steps - 1, 3, 24, width)
        b = b.reshape(steps - 1, 3, 24, width)
        part = join_cores(a, b, 48, 2).transpose(1, 0, 2, 3)[:, :, None]
        qkv_all = put(qkv_all, part, (0, 1, quad ^ n, 0, 0))
    qkv_all = qkv_all.reshape(3, width, width)

    own_rest = jnp.concatenate(
        [
            index_dim(index_dim(w_in, core, 0), quad, 0),
            core_rows(index_dim(w_out, quad, 0), core, 0),
            core_rows(index_dim(w_attn, quad, 0), core, 0),
        ],
        axis=0,
    )
    mine, theirs = gather_pieces(own_rest)
    in_all = jnp.zeros((2, steps, 4, 72, width), bf16).at[:, 0].set(w_in)
    out_all = jnp.zeros((steps, 4, 72, width), bf16).at[0].set(w_out)
    attn_all = jnp.zeros((steps, 4, 48, width), bf16).at[0].set(w_attn)
    for n in range(4):
        a, b = by_core(mine[n], theirs[n], core)
        pair = jnp.stack([a[:, :72], b[:, :72]])[:, :, None]
        in_all = put(in_all, pair, (0, 1, quad ^ n, 0, 0))
        out_all = put(
            out_all, join_cores(a[:, 72:112], b[:, 72:112], 72, 1)[:, None], (1, quad ^ n, 0, 0)
        )
        attn_all = put(
            attn_all, join_cores(a[:, 112:], b[:, 112:], 48, 1)[:, None], (1, quad ^ n, 0, 0)
        )
    ff = steps * 288
    in_all = in_all.reshape(2, ff, width)
    out_all = out_all.reshape(ff, width)
    attn_all = attn_all.reshape(width, width)

    cos, sin, bias = tables(seg_ids, here * rows, rows)
    gain_one = norm1_gain[None]
    gain_two = norm2_gain[None]
    low_one, q, k, v = qkv_call(x_ext, gain_one, qkv_all, cos, sin)
    low_attn, lse = attend_call(q, k, v, bias, rows)
    result, grad_mid, low_mid, dattn, low_two, low_act, ggu, gain_two_part = mlp_call(
        hidden_in, out_grad, low_attn, gain_two, attn_all, in_all, out_all
    )

    g_in = tn(ggu, low_two).astype(bf16).reshape(2, steps, 4, 72, width)
    g_out = tn(low_act, out_grad).astype(bf16).reshape(steps, 4, 72, width)
    g_attn = tn(low_attn, low_mid).astype(bf16).reshape(steps, 4, 48, width)

    def rest_for(c):
        return jnp.concatenate(
            [index_dim(g_in, c, 0), core_rows(g_out, c, 2), core_rows(g_attn, c, 2)], axis=2
        )

    rest = reduce_pieces(rest_for(1 - core), rest_for(core), quad)

    dq, dk, dv, edges = attend_back_call(q, k, v, dattn, bias, lse, cos, sin)
    got = pair_swap(jnp.where(odd, edges[:HALF], edges[HALF:])).reshape(HALF, 2, width)
    turn = width // steps
    got = jnp.where(odd, jnp.roll(got, turn, 2), jnp.roll(got, -turn, 2)).reshape(HALF, 2 * width)
    none = jnp.zeros_like(got)
    own = slice(HALF, HALF + rows)
    mix = mixed_call(
        dq,
        dk[own],
        dv[own],
        jnp.where(odd, got, none),
        jnp.where(odd, none, got),
        cos[own],
        sin[own],
    )
    g_qkv = tn(mix, low_one[own]).astype(bf16).reshape(3, steps, 4, 48, width)

    def qkv_for(c):
        part = core_rows(g_qkv, c, 3).transpose(1, 2, 0, 3, 4)
        return part.reshape(steps, 4, 72, width)

    qkv_total = reduce_pieces(qkv_for(1 - core), qkv_for(core), quad)
    grad_hidden, gain_one_part = input_grad_call(
        mix, qkv_all.reshape(3 * width, width), hidden_in, grad_mid, gain_one
    )

    gains = jnp.stack([jnp.sum(gain_one_part, axis=0), jnp.sum(gain_two_part, axis=0)])
    gains = jnp.pad(gains, ((0, 6), (0, 0)))
    mask = 1
    while mask < steps:
        gains = gains + lax.ppermute(gains, "tensor", [(i, i ^ mask) for i in range(steps)])
        mask *= 2
    mask = 1
    while mask < lax.axis_size("dp"):
        gains = gains + dp_swap(gains, mask)
        mask *= 2

    mine, theirs = spread_quads(rest[None])
    o_in = jnp.zeros((2, 4, 72, width), f32)
    o_out = jnp.zeros((4, 72, width), f32)
    o_attn = jnp.zeros((4, 48, width), f32)
    for n in range(4):
        a, b = by_core(mine[n][0].astype(f32), theirs[n][0].astype(f32), core)
        o_in = put(o_in, jnp.stack([a[:72], b[:72]])[:, None], (0, quad ^ n, 0, 0))
        o_out = put(o_out, join_cores(a[72:112], b[72:112], 72, 0)[None], (quad ^ n, 0, 0))
        o_attn = put(o_attn, join_cores(a[112:], b[112:], 48, 0)[None], (quad ^ n, 0, 0))
    mine, theirs = spread_quads(qkv_total[None])
    o_qkv = jnp.zeros((3, 4, 48, width), f32)
    for n in range(4):
        a, b = by_core(mine[n][0].astype(f32), theirs[n][0].astype(f32), core)
        part = join_cores(a.reshape(3, 24, width), b.reshape(3, 24, width), 48, 1)
        o_qkv = put(o_qkv, part[:, None], (0, quad ^ n, 0, 0))
    grad_qkv = o_qkv.reshape(3, 3, 64, width).transpose(3, 0, 1, 2)
    grad_in = o_in.reshape(2, 288, width).transpose(2, 0, 1)
    return (
        result,
        grad_hidden,
        gains[0],
        gains[1],
        grad_qkv,
        o_attn.reshape(192, width),
        grad_in,
        o_out.reshape(288, width),
    )


def solution(mesh):
    rows = P(("dp", "tensor"), None)
    in_specs = (
        rows,
        P("dp"),
        P(),
        P(),
        P(None, None, "tensor", None),
        P("tensor", None),
        P(None, None, "tensor"),
        P("tensor", None),
        rows,
    )
    out_specs = (
        rows,
        rows,
        P(),
        P(),
        P(None, None, "tensor", None),
        P("tensor", None),
        P(None, None, "tensor"),
        P("tensor", None),
    )
    return jax.shard_map(body, mesh=mesh, in_specs=in_specs, out_specs=out_specs, check_vma=False)
```

```python
import functools

import jax
import jax.numpy as jnp
from jax import lax
from jax.experimental import pallas as pl
from jax.experimental.pallas import tpu as pltpu
from jax.sharding import PartitionSpec as P

WINDOW = 128
HALF = WINDOW // 2
EPS = 1e-05
ROPE_BASE = 10000.0
BLK = 128
CORE, XBIT, YBIT = 1, 2, 4
bf16 = jnp.bfloat16
f32 = jnp.float32
MIB = 1024 * 1024


def nn(a, b):
    return lax.dot_general(a, b, (((1,), (0,)), ((), ())), preferred_element_type=f32)


def nt(a, b):
    return lax.dot_general(a, b, (((1,), (1,)), ((), ())), preferred_element_type=f32)


def tn(a, b):
    return lax.dot_general(a, b, (((0,), (0,)), ((), ())), preferred_element_type=f32)


def row_stats(x):
    mean = jnp.mean(x, axis=-1, keepdims=True)
    cen = x - mean
    inv = lax.rsqrt(jnp.mean(cen * cen, axis=-1, keepdims=True) + EPS)
    return cen * inv, inv


def fold_rows(x):
    return jnp.sum(x.reshape(x.shape[0] // 8, 8, x.shape[1]), axis=0)


def const_spec(shape):
    zeros = (0,) * len(shape)
    return pl.BlockSpec(shape, lambda i: zeros, pipeline_mode=pl.Buffered(1))


def row_spec(rows, cols):
    return pl.BlockSpec((rows, cols), lambda i: (i, 0))


def params(mib):
    return pltpu.CompilerParams(
        dimension_semantics=("arbitrary",), vmem_limit_bytes=mib * MIB
    )


def turn_lanes(z, lo_sign):
    width = z.shape[1]
    lane = lax.broadcasted_iota(jnp.int32, (1, width), 1)
    first = lane % 64 < 32
    ahead = pltpu.roll(z, width - 32, 1)
    behind = pltpu.roll(z, 32, 1)
    return jnp.where(first, lo_sign * ahead, -lo_sign * behind)


def qkv_kernel(x_ref, gain_ref, w_ref, cos_ref, sin_ref, low_ref, q_ref, k_ref, v_ref):
    normed, _ = row_stats(x_ref[...].astype(f32))
    low = (normed * gain_ref[...]).astype(bf16)
    low_ref[...] = low
    width = low.shape[1]
    cos = jnp.concatenate([cos_ref[...]] * (width // 128), axis=1)
    sin = jnp.concatenate([sin_ref[...]] * (width // 128), axis=1)
    q = nt(low, w_ref[0])
    q_ref[...] = (q * cos + turn_lanes(q, -1.0) * sin).astype(bf16)
    k = nt(low, w_ref[1])
    k_ref[...] = (k * cos + turn_lanes(k, -1.0) * sin).astype(bf16)
    v_ref[...] = nt(low, w_ref[2]).astype(bf16)


def qkv_call(x_ext, gain, w, cos, sin):
    rows, width = x_ext.shape
    blk = rows // 3
    out = jax.ShapeDtypeStruct((rows, width), bf16)
    return pl.pallas_call(
        qkv_kernel,
        grid=(rows // blk,),
        in_specs=[
            row_spec(blk, width),
            const_spec((1, width)),
            const_spec(w.shape),
            row_spec(blk, 128),
            row_spec(blk, 128),
        ],
        out_specs=[row_spec(blk, width)] * 4,
        out_shape=[out] * 4,
        compiler_params=params(40),
        cost_estimate=pl.CostEstimate(
            flops=6 * rows * width * width, bytes_accessed=14 * MIB, transcendentals=0
        ),
        name="qkv",
    )(x_ext, gain, w, cos, sin)


def stack_pair(z, scale):
    lane = lax.broadcasted_iota(jnp.int32, (1, 128), 1)
    low_head = (lane < 64).astype(f32) * scale
    high_head = (lane >= 64).astype(f32) * scale
    return jnp.concatenate([z * low_head.astype(bf16), z * high_head.astype(bf16)], axis=0)


def merge_pair(z):
    rows = z.shape[0] // 2
    lane = lax.broadcasted_iota(jnp.int32, (1, 128), 1)
    return jnp.where(lane < 64, z[:rows], z[rows:])


def attend_kernel(q_ref, k_ref, v_ref, bias_ref, out_ref, lse_ref):
    b = pl.program_id(0)
    start = pl.multiple_of(b * BLK, BLK)
    bias = bias_ref[0]
    bias = jnp.concatenate([bias, bias], axis=1)
    for j in range(q_ref.shape[1] // 128):
        cols = slice(128 * j, 128 * j + 128)
        qs = stack_pair(q_ref[pl.ds(start + HALF, BLK), cols], 0.125)
        kb = k_ref[pl.ds(start, 2 * BLK), cols]
        vb = v_ref[pl.ds(start, 2 * BLK), cols]
        s = nt(kb, qs) + bias
        top = jnp.max(s, axis=0, keepdims=True)
        e = jnp.exp(s - top)
        total = jnp.sum(e, axis=0, keepdims=True)
        low_p = (e * (1.0 / total)).astype(bf16)
        out_ref[:, cols] = merge_pair(tn(low_p, vb)).astype(bf16)
        lse_ref[0, j : j + 1, :] = top + jnp.log(total)


def attend_call(q, k, v, bias, rows):
    ext, width = q.shape
    blocks = rows // BLK
    return pl.pallas_call(
        attend_kernel,
        grid=(blocks,),
        in_specs=[
            const_spec((ext, width)),
            const_spec((ext, width)),
            const_spec((ext, width)),
            pl.BlockSpec((1, 2 * BLK, BLK), lambda i: (i, 0, 0)),
        ],
        out_specs=[row_spec(BLK, width), pl.BlockSpec((1, 8, 2 * BLK), lambda i: (i, 0, 0))],
        out_shape=[
            jax.ShapeDtypeStruct((rows, width), bf16),
            jax.ShapeDtypeStruct((blocks, 8, 2 * BLK), f32),
        ],
        compiler_params=params(32),
        cost_estimate=pl.CostEstimate(
            flops=12 * rows * 256 * width, bytes_accessed=9 * MIB, transcendentals=rows * 3072
        ),
        name="attend",
    )(q, k, v, bias)


def mlp_kernel(
    x_ref,
    og_ref,
    attn_ref,
    gain_ref,
    wa_ref,
    wi_ref,
    wo_ref,
    out_ref,
    gmid_ref,
    lowmid_ref,
    dattn_ref,
    low2_ref,
    act_ref,
    ggu_ref,
    gain_grad_ref,
):
    gain = gain_ref[...]
    middle = x_ref[...].astype(f32) + nn(attn_ref[...], wa_ref[...])
    normed, inv = row_stats(middle)
    low_two = (normed * gain).astype(bf16)
    low2_ref[...] = low_two
    og = og_ref[...]
    ff = wo_ref.shape[0]
    chunk = 384
    result = middle
    grad_n = jnp.zeros(middle.shape, f32)
    for c in range(ff // chunk):
        sl = slice(c * chunk, c * chunk + chunk)
        gate = nt(low_two, wi_ref[0, sl])
        up = nt(low_two, wi_ref[1, sl])
        wo = wo_ref[sl]
        phi = 0.5 + 0.5 * lax.erf(gate * (0.5**0.5))
        gel = gate * phi
        act = (gel * up).astype(bf16)
        act_ref[:, sl] = act
        result = result + nn(act, wo)
        grad_act = nt(og, wo)
        dens = jnp.exp(-0.5 * gate * gate) * 0.3989422804014327
        g_gate = (grad_act * up * (phi + gate * dens)).astype(bf16)
        g_up = (grad_act * gel).astype(bf16)
        ggu_ref[:, sl] = g_gate
        ggu_ref[:, ff + c * chunk : ff + c * chunk + chunk] = g_up
        grad_n = grad_n + nn(g_gate, wi_ref[0, sl]) + nn(g_up, wi_ref[1, sl])
    out_ref[...] = result.astype(bf16)

    @pl.when(pl.program_id(0) == 0)
    def _():
        gain_grad_ref[...] = jnp.zeros(gain_grad_ref.shape, f32)

    gain_grad_ref[...] += fold_rows(grad_n * normed)
    u = grad_n * gain
    grad_mid = og.astype(f32) + inv * (
        u
        - jnp.mean(u, axis=-1, keepdims=True)
        - normed * jnp.mean(u * normed, axis=-1, keepdims=True)
    )
    gmid_ref[...] = grad_mid
    low_mid = grad_mid.astype(bf16)
    lowmid_ref[...] = low_mid
    dattn_ref[...] = nt(low_mid, wa_ref[...]).astype(bf16)


def mlp_call(x, og, attn, gain, wa, wi, wo):
    rows, width = x.shape
    ff = wo.shape[0]
    blk = 256
    low = jax.ShapeDtypeStruct((rows, width), bf16)
    return pl.pallas_call(
        mlp_kernel,
        grid=(rows // blk,),
        in_specs=[row_spec(blk, width)] * 3
        + [const_spec((1, width)), const_spec(wa.shape), const_spec(wi.shape), const_spec(wo.shape)],
        out_specs=[row_spec(blk, width)] * 5
        + [row_spec(blk, ff), row_spec(blk, 2 * ff), pl.BlockSpec((8, width), lambda i: (0, 0))],
        out_shape=[
            low,
            jax.ShapeDtypeStruct((rows, width), f32),
            low,
            low,
            low,
            jax.ShapeDtypeStruct((rows, ff), bf16),
            jax.ShapeDtypeStruct((rows, 2 * ff), bf16),
            jax.ShapeDtypeStruct((8, width), f32),
        ],
        compiler_params=params(48),
        cost_estimate=pl.CostEstimate(
            flops=4 * rows * width * (width + 3 * ff),
            bytes_accessed=30 * MIB,
            transcendentals=2 * rows * ff,
        ),
        name="mlp",
    )(x, og, attn, gain, wa, wi, wo)


def attend_back_kernel(
    first_pair,
    q_ref,
    k_ref,
    v_ref,
    do_ref,
    bias_ref,
    lse_ref,
    cos_ref,
    sin_ref,
    dq_ref,
    dk_ref,
    dv_ref,
    edge_ref,
):
    b = pl.program_id(0)
    start = pl.multiple_of(b * BLK, BLK)

    @pl.when(b == 0)
    def _():
        dk_ref[...] = jnp.zeros(dk_ref.shape, f32)
        dv_ref[...] = jnp.zeros(dv_ref.shape, f32)

    bias = bias_ref[0]
    bias = jnp.concatenate([bias, bias], axis=1)
    rows = pl.ds(start, 2 * BLK)
    cos = cos_ref[pl.ds(start + HALF, BLK), :] * 0.125
    sin = sin_ref[pl.ds(start + HALF, BLK), :] * 0.125
    for j in range(q_ref.shape[1] // 128):
        cols = slice(128 * j, 128 * j + 128)
        qs = stack_pair(q_ref[pl.ds(start + HALF, BLK), cols], 0.125)
        dos = stack_pair(do_ref[:, cols], 1.0)
        kb = k_ref[rows, cols]
        vb = v_ref[rows, cols]
        p = jnp.exp(nt(kb, qs) + bias - lse_ref[0, first_pair + j : first_pair + j + 1, :])
        dp = nt(vb, dos)
        dot = jnp.sum(p * dp, axis=0, keepdims=True)
        ds = (p * (dp - dot)).astype(bf16)
        dv_ref[rows, cols] += nn(p.astype(bf16), dos)
        dk_ref[rows, cols] += nn(ds, qs)
        dq = merge_pair(tn(ds, kb))
        dq_ref[:, cols] = (dq * cos + turn_lanes(dq * sin, 1.0)).astype(bf16)

    @pl.when(b == pl.num_programs(0) - 1)
    def _():
        width = dk_ref.shape[1]
        ext = dk_ref.shape[0]
        for at, ref in ((0, dk_ref), (width, dv_ref)):
            edge_ref[:HALF, at : at + width] = ref[:HALF, :].astype(bf16)
            edge_ref[HALF:, at : at + width] = ref[ext - HALF :, :].astype(bf16)


def attend_back_call(q, k, v, do, bias, lse, cos, sin, at):
    ext = q.shape[0]
    width = q.shape[1] // 2
    rows = do.shape[0]
    full = pl.BlockSpec((ext, width), lambda i: (0, at), pipeline_mode=pl.Buffered(1))
    acc = pl.BlockSpec((ext, width), lambda i: (0, 0))
    return pl.pallas_call(
        functools.partial(attend_back_kernel, at * (width // 128)),
        grid=(rows // BLK,),
        in_specs=[
            full,
            full,
            full,
            pl.BlockSpec((BLK, width), lambda i: (i, at)),
            pl.BlockSpec((1, 2 * BLK, BLK), lambda i: (i, 0, 0)),
            pl.BlockSpec((1, 8, 2 * BLK), lambda i: (i, 0, 0)),
            const_spec((ext, 128)),
            const_spec((ext, 128)),
        ],
        out_specs=[
            row_spec(BLK, width),
            acc,
            acc,
            pl.BlockSpec((WINDOW, 2 * width), lambda i: (0, 0)),
        ],
        out_shape=[
            jax.ShapeDtypeStruct((rows, width), bf16),
            jax.ShapeDtypeStruct((ext, width), f32),
            jax.ShapeDtypeStruct((ext, width), f32),
            jax.ShapeDtypeStruct((WINDOW, 2 * width), bf16),
        ],
        compiler_params=params(48),
        cost_estimate=pl.CostEstimate(
            flops=30 * rows * 256 * width, bytes_accessed=20 * MIB, transcendentals=rows * 3072
        ),
        name="attend_back",
    )(q, k, v, do, bias, lse, cos, sin)


def mixed_kernel(
    dq0_ref, dq1_ref, dk0_ref, dk1_ref, dv0_ref, dv1_ref, first_ref, last_ref, cos_ref, sin_ref, mix_ref
):
    rows = mix_ref.shape[0]
    part = dq0_ref.shape[1]
    width = 2 * part
    i = pl.program_id(0)
    own = pl.ds(pl.multiple_of(i * rows, rows) + HALF, rows)
    cos = jnp.concatenate([cos_ref[own, :]] * (part // 128), axis=1)
    sin = jnp.concatenate([sin_ref[own, :]] * (part // 128), axis=1)
    pad = jnp.zeros((rows - HALF, part), f32)
    is_first = (i == 0).astype(f32)
    is_last = (i == pl.num_programs(0) - 1).astype(f32)

    def joined(ref, at):
        cols = slice(at, at + part)
        head = first_ref[:, cols].astype(f32) * is_first
        tail = last_ref[:, cols].astype(f32) * is_last
        return ref[own, :] + jnp.concatenate([head, pad], axis=0) + jnp.concatenate([pad, tail], axis=0)

    for h, (dq_ref, dk_ref, dv_ref) in enumerate(
        ((dq0_ref, dk0_ref, dv0_ref), (dq1_ref, dk1_ref, dv1_ref))
    ):
        at = h * part
        mix_ref[:, at : at + part] = dq_ref[...]
        dk = joined(dk_ref, at)
        dk = (dk * cos + turn_lanes(dk * sin, 1.0)).astype(bf16)
        mix_ref[:, width + at : width + at + part] = dk
        dv = joined(dv_ref, width + at)
        mix_ref[:, 2 * width + at : 2 * width + at + part] = dv.astype(bf16)


def mixed_call(halves, first, last, cos, sin):
    (dq0, dk0, dv0), (dq1, dk1, dv1) = halves
    rows, part = dq0.shape
    blk = 256
    full = const_spec(dk0.shape)
    table = const_spec(cos.shape)
    return pl.pallas_call(
        mixed_kernel,
        grid=(rows // blk,),
        in_specs=[row_spec(blk, part)] * 2
        + [full] * 4
        + [const_spec(first.shape), const_spec(last.shape)]
        + [table] * 2,
        out_specs=row_spec(blk, 6 * part),
        out_shape=jax.ShapeDtypeStruct((rows, 6 * part), bf16),
        compiler_params=params(32),
        cost_estimate=pl.CostEstimate(
            flops=20 * rows * part, bytes_accessed=14 * MIB, transcendentals=0
        ),
        name="mixed",
    )(dq0, dq1, dk0, dk1, dv0, dv1, first, last, cos, sin)


def input_grad_kernel(mix_ref, w_ref, x_ref, gmid_ref, gain_ref, out_ref, gain_grad_ref):
    grad_n = nn(mix_ref[...], w_ref[...])
    normed, inv = row_stats(x_ref[...].astype(f32))

    @pl.when(pl.program_id(0) == 0)
    def _():
        gain_grad_ref[...] = jnp.zeros(gain_grad_ref.shape, f32)

    gain_grad_ref[...] += fold_rows(grad_n * normed)
    u = grad_n * gain_ref[...]
    out_ref[...] = (
        gmid_ref[...]
        + inv
        * (
            u
            - jnp.mean(u, axis=-1, keepdims=True)
            - normed * jnp.mean(u * normed, axis=-1, keepdims=True)
        )
    ).astype(bf16)


def input_grad_call(mix, w, x, gmid, gain):
    rows, width = x.shape
    blk = 256
    return pl.pallas_call(
        input_grad_kernel,
        grid=(rows // blk,),
        in_specs=[
            row_spec(blk, 3 * width),
            const_spec(w.shape),
            row_spec(blk, width),
            row_spec(blk, width),
            const_spec((1, width)),
        ],
        out_specs=[row_spec(blk, width), pl.BlockSpec((8, width), lambda i: (0, 0))],
        out_shape=[
            jax.ShapeDtypeStruct((rows, width), bf16),
            jax.ShapeDtypeStruct((8, width), f32),
        ],
        compiler_params=params(40),
        cost_estimate=pl.CostEstimate(
            flops=6 * rows * width * width, bytes_accessed=16 * MIB, transcendentals=0
        ),
        name="input_grad",
    )(mix, w, x, gmid, gain)


def dp_swap(x, mask):
    count = lax.axis_size("dp")
    return lax.ppermute(x, "dp", [(i, i ^ mask) for i in range(count)])


def ring_shift(x, step):
    count = lax.axis_size("tensor")
    return lax.ppermute(x, "tensor", [(i, (i + step) % count) for i in range(count)])


def pair_swap(x):
    count = lax.axis_size("tensor")
    return lax.ppermute(x, "tensor", [(i, i ^ 1) for i in range(count)])


def index_dim(x, at, dim):
    return lax.squeeze(lax.dynamic_slice_in_dim(x, at, 1, dim), (dim,))


def core_rows(x, core, dim):
    rows = x.shape[dim]
    size = (rows // 2 + 7) // 8 * 8
    step = (rows - size) // 8
    tiles = x.reshape(x.shape[:dim] + (rows // 8, 8) + x.shape[dim + 1 :])
    part = lax.dynamic_slice_in_dim(tiles, core * step, size // 8, dim)
    return part.reshape(x.shape[:dim] + (size,) + x.shape[dim + 1 :])


def join_cores(a, b, rows, dim):
    size = a.shape[dim]
    keep = rows - size
    return jnp.concatenate([a, lax.slice_in_dim(b, size - keep, size, axis=dim)], axis=dim)


def hold(value, *after):
    return lax.optimization_barrier((value,) + after)[0]


def spread_quads(piece):
    half = (piece.shape[1] // 2 + 7) // 8 * 8
    from_x = dp_swap(piece, XBIT)
    from_y = dp_swap(piece, YBIT)
    return piece, from_x, from_y, half


def spread_diag(piece, from_x, from_y, half):
    diag_x = dp_swap(from_y[:, :half], XBIT)
    diag_y = dp_swap(from_x[:, half:], YBIT)
    early = dp_swap(jnp.stack([piece, from_x, from_y]), CORE)
    return early, diag_x, diag_y


def spread_core(piece, from_x, from_y, early, diag_x, diag_y):
    diag = jnp.concatenate([diag_x, diag_y], axis=1)
    late = dp_swap(diag, CORE)
    return [piece, from_x, from_y, diag], [early[0], early[1], early[2], late]


def spread_all(piece):
    piece, from_x, from_y, half = spread_quads(piece)
    return spread_core(piece, from_x, from_y, *spread_diag(piece, from_x, from_y, half))


def ring_pieces(piece):
    return jnp.stack([ring_shift(piece, s) for s in range(1, lax.axis_size("tensor"))])


def by_core(mine, theirs, core):
    first = core == 0
    return jnp.where(first, mine, theirs), jnp.where(first, theirs, mine)


def add(a, b):
    return (a.astype(f32) + b.astype(f32)).astype(bf16)


def halve(arr, at, mask, dim):
    got = dp_swap(index_dim(arr, 1 - at, dim), mask)
    return index_dim(arr, at, dim), got


def reduce_core(send, keep):
    return add(keep, dp_swap(send, CORE))


def reduce_first(total, quad):
    steps, _, rows, width = total.shape
    grid = total.reshape(steps, 2, 2, rows, width)
    half = steps // 2
    return halve(grid[:half], quad & 1, XBIT, 2) + halve(grid[half:], quad >> 1, YBIT, 1)


def reduce_second(keep_x, got_x, keep_y, got_y, quad):
    first = add(keep_x, got_x)
    second = add(keep_y, got_y)
    return halve(first, quad >> 1, YBIT, 1) + halve(second, quad & 1, XBIT, 1)


def reduce_ring(keep_y, got_y, keep_x, got_x):
    first = add(keep_y, got_y)
    second = add(keep_x, got_x)
    half = first.shape[0]
    steps = half + second.shape[0]
    parts = [first[s] for s in range(half)] + [second[s] for s in range(steps - half)]
    mask = 8
    if lax.axis_size("dp") > mask:
        block = jnp.stack(parts)
        while mask < lax.axis_size("dp"):
            block = add(block, dp_swap(block, mask))
            mask *= 2
        parts = [block[s] for s in range(steps)]
    return [parts[0]] + [ring_shift(parts[s], -s) for s in range(1, steps)]


def reduce_sum(parts):
    result = parts[0].astype(f32)
    for part in parts[1:]:
        result = result + part.astype(f32)
    return result.astype(bf16)


def put(buf, part, starts):
    return lax.dynamic_update_slice(buf, part, starts)


def tables(seg_ids, first_row, rows):
    count = seg_ids.shape[0]
    places = jnp.arange(count, dtype=jnp.int32)
    earlier = jnp.concatenate([jnp.full((1,), -1, jnp.int32), seg_ids[:-1]])
    starts = jnp.where(seg_ids != earlier, places, 0)
    positions = places - lax.cummax(starts, axis=0)
    ext = rows + WINDOW
    seg_ext = lax.dynamic_slice(jnp.pad(seg_ids, HALF, constant_values=-1), (first_row,), (ext,))
    pos_ext = lax.dynamic_slice(jnp.pad(positions, HALF), (first_row,), (ext,))
    freq = ROPE_BASE ** (-jnp.arange(0, 64, 2).astype(f32) / 64)
    angles = pos_ext.astype(f32)[:, None] * jnp.concatenate([freq] * 4)[None, :]
    blocks = rows // BLK
    seg_rows = seg_ext.reshape(blocks + 1, BLK)
    seg_k = jnp.concatenate([seg_rows[:-1], seg_rows[1:]], axis=1)
    seg_q = seg_ext[HALF : HALF + rows].reshape(blocks, BLK)
    k_place = jnp.arange(2 * BLK, dtype=jnp.int32)[:, None] - HALF
    q_place = jnp.arange(BLK, dtype=jnp.int32)[None, :]
    near = jnp.abs(k_place - q_place) <= HALF
    allowed = near[None] & (seg_k[:, :, None] == seg_q[:, None, :])
    bias = jnp.where(allowed, 0.0, -1e30).astype(f32)
    return jnp.cos(angles), jnp.sin(angles), bias


def body(
    hidden_in,
    seg_ids,
    norm1_gain,
    norm2_gain,
    qkv_weight,
    attn_weight,
    mlp_in_weight,
    mlp_out_weight,
    out_grad,
):
    rows, width = hidden_in.shape
    steps = lax.axis_size("tensor")
    here = lax.axis_index("tensor")
    at_dp = lax.axis_index("dp")
    core = at_dp & 1
    quad = (at_dp >> 1) & 3
    odd = (here & 1) == 1
    w_qkv = qkv_weight.transpose(1, 2, 3, 0).reshape(3, 4, 48, width)
    w_in = mlp_in_weight.transpose(1, 2, 0).reshape(2, 4, 72, width)
    w_out = mlp_out_weight.reshape(4, 72, width)
    w_attn = attn_weight.reshape(4, 48, width)

    edge = jnp.where(odd, hidden_in[:HALF], hidden_in[-HALF:])
    halo = pair_swap(edge)
    none = jnp.zeros_like(halo)
    x_ext = jnp.concatenate(
        [jnp.where(odd, halo, none), hidden_in, jnp.where(odd, none, halo)], axis=0
    )

    own_qkv = core_rows(index_dim(w_qkv, quad, 1), core, 1).reshape(3 * 24, width)
    own_rest = jnp.concatenate(
        [
            index_dim(index_dim(w_in, core, 0), quad, 0),
            core_rows(index_dim(w_out, quad, 0), core, 0),
            core_rows(index_dim(w_attn, quad, 0), core, 0),
        ],
        axis=0,
    )
    ring_qkv = ring_pieces(own_qkv)
    ring_rest = ring_pieces(hold(own_rest, own_qkv))

    quads_qkv = spread_quads(ring_qkv)
    diag_qkv = spread_diag(*quads_qkv)
    quads_rest = spread_quads(hold(ring_rest, quads_qkv[1], quads_qkv[2]))
    mine, theirs = spread_core(*quads_qkv[:3], *diag_qkv)
    qkv_all = jnp.zeros((3, steps, 4, 48, width), bf16)
    qkv_all = qkv_all.at[:, 0].set(w_qkv)
    for n in range(4):
        a, b = by_core(mine[n], theirs[n], core)
        a = a.reshape(steps - 1, 3, 24, width)
        b = b.reshape(steps - 1, 3, 24, width)
        part = join_cores(a, b, 48, 2).transpose(1, 0, 2, 3)[:, :, None]
        qkv_all = put(qkv_all, part, (0, 1, quad ^ n, 0, 0))
    qkv_all = qkv_all.reshape(3, width, width)

    cos, sin, bias = tables(seg_ids, here * rows, rows)
    gain_one = norm1_gain[None]
    gain_two = norm2_gain[None]
    low_one, q, k, v = qkv_call(x_ext, gain_one, hold(qkv_all, ring_rest), cos, sin)
    low_attn, lse = attend_call(hold(q, *quads_rest[1:3]), k, v, bias, rows)

    diag_rest = spread_diag(*quads_rest)
    mine, theirs = spread_core(*quads_rest[:3], *diag_rest)
    in_all = jnp.zeros((2, steps, 4, 72, width), bf16).at[:, 0].set(w_in)
    out_all = jnp.zeros((steps, 4, 72, width), bf16).at[0].set(w_out)
    attn_all = jnp.zeros((steps, 4, 48, width), bf16).at[0].set(w_attn)
    for n in range(4):
        a, b = by_core(mine[n], theirs[n], core)
        pair = jnp.stack([a[:, :72], b[:, :72]])[:, :, None]
        in_all = put(in_all, pair, (0, 1, quad ^ n, 0, 0))
        out_all = put(
            out_all, join_cores(a[:, 72:112], b[:, 72:112], 72, 1)[:, None], (1, quad ^ n, 0, 0)
        )
        attn_all = put(
            attn_all, join_cores(a[:, 112:], b[:, 112:], 48, 1)[:, None], (1, quad ^ n, 0, 0)
        )
    ff = steps * 288
    in_all = in_all.reshape(2, ff, width)
    out_all = out_all.reshape(ff, width)
    attn_all = attn_all.reshape(width, width)

    result, grad_mid, low_mid, dattn, low_two, low_act, ggu, gain_two_part = mlp_call(
        hidden_in, out_grad, low_attn, gain_two, attn_all, in_all, out_all
    )

    g_in = tn(ggu, low_two).astype(bf16).reshape(2, steps, 4, 72, width)
    g_out = tn(low_act, out_grad).astype(bf16).reshape(steps, 4, 72, width)
    g_attn = tn(low_attn, low_mid).astype(bf16).reshape(steps, 4, 48, width)

    def rest_for(c):
        return jnp.concatenate(
            [index_dim(g_in, c, 0), core_rows(g_out, c, 2), core_rows(g_attn, c, 2)], axis=2
        )

    send, keep = rest_for(1 - core), rest_for(core)
    dattn = hold(dattn, send)
    back_first = attend_back_call(q, k, v, dattn, bias, lse, cos, sin, 0)
    core_rest = reduce_core(send, keep)
    first_rest = reduce_first(core_rest, quad)
    dattn = hold(dattn, core_rest, back_first[0])
    back_second = attend_back_call(q, k, v, dattn, bias, lse, cos, sin, 1)
    part = width // 2
    edges = jnp.concatenate(
        [
            back_first[3][:, :part],
            back_second[3][:, :part],
            back_first[3][:, part:],
            back_second[3][:, part:],
        ],
        axis=1,
    )
    got = pair_swap(jnp.where(odd, edges[:HALF], edges[HALF:])).reshape(HALF, 2, width)
    turn = width // steps
    got = jnp.where(odd, jnp.roll(got, turn, 2), jnp.roll(got, -turn, 2)).reshape(HALF, 2 * width)
    none = jnp.zeros_like(got)
    own = slice(HALF, HALF + rows)
    mix = mixed_call(
        (back_first[:3], back_second[:3]),
        jnp.where(odd, got, none),
        jnp.where(odd, none, got),
        cos,
        sin,
    )
    g_qkv = tn(mix, low_one[HALF : HALF + rows]).astype(bf16).reshape(3, steps, 4, 48, width)

    def qkv_for(c):
        part = core_rows(g_qkv, c, 3).transpose(1, 2, 0, 3, 4)
        return part.reshape(steps, 4, 72, width)

    send_qkv, keep_qkv = qkv_for(1 - core), qkv_for(core)
    second_rest = reduce_second(*first_rest, quad)
    grad_hidden, gain_one_part = input_grad_call(
        hold(mix, send_qkv, *second_rest[::2]),
        qkv_all.reshape(3 * width, width),
        hidden_in,
        grad_mid,
        gain_one,
    )
    core_qkv = reduce_core(send_qkv, keep_qkv)
    first_qkv = reduce_first(core_qkv, quad)
    ring_back = reduce_ring(*second_rest)
    second_qkv = reduce_second(*first_qkv, quad)
    rest = reduce_sum(ring_back)
    qkv_total = reduce_sum(reduce_ring(*second_qkv))

    gains = jnp.stack([jnp.sum(gain_one_part, axis=0), jnp.sum(gain_two_part, axis=0)])
    gains = jnp.pad(gains, ((0, 6), (0, 0)))
    mask = 1
    while mask < steps:
        gains = gains + lax.ppermute(gains, "tensor", [(i, i ^ mask) for i in range(steps)])
        mask *= 2
    mask = 1
    while mask < lax.axis_size("dp"):
        gains = gains + dp_swap(gains, mask)
        mask *= 2

    mine, theirs = spread_all(jnp.concatenate([rest, qkv_total])[None])
    cut = rest.shape[0]
    o_in = jnp.zeros((2, 4, 72, width), f32)
    o_out = jnp.zeros((4, 72, width), f32)
    o_attn = jnp.zeros((4, 48, width), f32)
    o_qkv = jnp.zeros((3, 4, 48, width), f32)
    for n in range(4):
        a, b = by_core(mine[n][0].astype(f32), theirs[n][0].astype(f32), core)
        o_in = put(o_in, jnp.stack([a[:72], b[:72]])[:, None], (0, quad ^ n, 0, 0))
        o_out = put(o_out, join_cores(a[72:112], b[72:112], 72, 0)[None], (quad ^ n, 0, 0))
        o_attn = put(o_attn, join_cores(a[112:cut], b[112:cut], 48, 0)[None], (quad ^ n, 0, 0))
        a = a[cut:].reshape(3, 24, width)
        b = b[cut:].reshape(3, 24, width)
        o_qkv = put(o_qkv, join_cores(a, b, 48, 1)[:, None], (0, quad ^ n, 0, 0))
    grad_qkv = o_qkv.reshape(3, 3, 64, width).transpose(3, 0, 1, 2)
    grad_in = o_in.reshape(2, 288, width).transpose(2, 0, 1)
    return (
        result,
        grad_hidden,
        gains[0],
        gains[1],
        grad_qkv,
        o_attn.reshape(192, width),
        grad_in,
        o_out.reshape(288, width),
    )


def solution(mesh):
    rows = P(("dp", "tensor"), None)
    in_specs = (
        rows,
        P("dp"),
        P(),
        P(),
        P(None, None, "tensor", None),
        P("tensor", None),
        P(None, None, "tensor"),
        P("tensor", None),
        rows,
    )
    out_specs = (
        rows,
        rows,
        P(),
        P(),
        P(None, None, "tensor", None),
        P("tensor", None),
        P(None, None, "tensor"),
        P("tensor", None),
    )
    return jax.shard_map(body, mesh=mesh, in_specs=in_specs, out_specs=out_specs, check_vma=False)
```

```python
import functools

import jax
import jax.numpy as jnp
from jax import lax
from jax.experimental import pallas as pl
from jax.experimental.pallas import tpu as pltpu
from jax.sharding import PartitionSpec as P

WINDOW = 128
HALF = WINDOW // 2
EPS = 1e-05
ROPE_BASE = 10000.0
BLK = 128
CORE, XBIT, YBIT = 1, 2, 4
bf16 = jnp.bfloat16
f32 = jnp.float32
MIB = 1024 * 1024
SMALL = pl.CostEstimate(flops=1000, bytes_accessed=1000, transcendentals=0)


def nn(a, b):
    return lax.dot_general(a, b, (((1,), (0,)), ((), ())), preferred_element_type=f32)


def nt(a, b):
    return lax.dot_general(a, b, (((1,), (1,)), ((), ())), preferred_element_type=f32)


def tn(a, b):
    return lax.dot_general(a, b, (((0,), (0,)), ((), ())), preferred_element_type=f32)


def row_stats(x):
    mean = jnp.mean(x, axis=-1, keepdims=True)
    cen = x - mean
    inv = lax.rsqrt(jnp.mean(cen * cen, axis=-1, keepdims=True) + EPS)
    return cen * inv, inv


def fold_rows(x):
    return jnp.sum(x.reshape(x.shape[0] // 8, 8, x.shape[1]), axis=0)


def const_spec(shape):
    zeros = (0,) * len(shape)
    return pl.BlockSpec(shape, lambda i: zeros, pipeline_mode=pl.Buffered(1))


def row_spec(rows, cols):
    return pl.BlockSpec((rows, cols), lambda i: (i, 0))


def params(mib):
    return pltpu.CompilerParams(
        dimension_semantics=("arbitrary",), vmem_limit_bytes=mib * MIB
    )


def turn_lanes(z, lo_sign):
    width = z.shape[1]
    lane = lax.broadcasted_iota(jnp.int32, (1, width), 1)
    first = lane % 64 < 32
    ahead = pltpu.roll(z, width - 32, 1)
    behind = pltpu.roll(z, 32, 1)
    return jnp.where(first, lo_sign * ahead, -lo_sign * behind)


def qkv_kernel(x_ref, gain_ref, w_ref, cos_ref, sin_ref, low_ref, q_ref, k_ref, v_ref):
    normed, _ = row_stats(x_ref[...].astype(f32))
    low = (normed * gain_ref[...]).astype(bf16)
    low_ref[...] = low
    width = low.shape[1]
    cos = jnp.concatenate([cos_ref[...]] * (width // 128), axis=1)
    sin = jnp.concatenate([sin_ref[...]] * (width // 128), axis=1)
    q = nt(low, w_ref[0])
    q_ref[...] = (q * cos + turn_lanes(q, -1.0) * sin).astype(bf16)
    k = nt(low, w_ref[1])
    k_ref[...] = (k * cos + turn_lanes(k, -1.0) * sin).astype(bf16)
    v_ref[...] = nt(low, w_ref[2]).astype(bf16)


def qkv_call(x_ext, gain, w, cos, sin):
    rows, width = x_ext.shape
    blk = rows // 3
    out = jax.ShapeDtypeStruct((rows, width), bf16)
    return pl.pallas_call(
        qkv_kernel,
        grid=(rows // blk,),
        in_specs=[
            row_spec(blk, width),
            const_spec((1, width)),
            const_spec(w.shape),
            row_spec(blk, 128),
            row_spec(blk, 128),
        ],
        out_specs=[row_spec(blk, width)] * 4,
        out_shape=[out] * 4,
        compiler_params=params(40),
        cost_estimate=SMALL,
        name="qkv",
    )(x_ext, gain, w, cos, sin)


def stack_pair(z, scale):
    lane = lax.broadcasted_iota(jnp.int32, (1, 128), 1)
    low_head = (lane < 64).astype(f32) * scale
    high_head = (lane >= 64).astype(f32) * scale
    return jnp.concatenate([z * low_head.astype(bf16), z * high_head.astype(bf16)], axis=0)


def merge_pair(z):
    rows = z.shape[0] // 2
    lane = lax.broadcasted_iota(jnp.int32, (1, 128), 1)
    return jnp.where(lane < 64, z[:rows], z[rows:])


def attend_kernel(q_ref, k_ref, v_ref, bias_ref, out_ref, lse_ref):
    b = pl.program_id(0)
    start = pl.multiple_of(b * BLK, BLK)
    bias = bias_ref[0]
    bias = jnp.concatenate([bias, bias], axis=1)
    for j in range(q_ref.shape[1] // 128):
        cols = slice(128 * j, 128 * j + 128)
        qs = stack_pair(q_ref[pl.ds(start + HALF, BLK), cols], 0.125)
        kb = k_ref[pl.ds(start, 2 * BLK), cols]
        vb = v_ref[pl.ds(start, 2 * BLK), cols]
        s = nt(kb, qs) + bias
        top = jnp.max(s, axis=0, keepdims=True)
        e = jnp.exp(s - top)
        total = jnp.sum(e, axis=0, keepdims=True)
        low_p = (e * (1.0 / total)).astype(bf16)
        out_ref[:, cols] = merge_pair(tn(low_p, vb)).astype(bf16)
        lse_ref[0, j : j + 1, :] = top + jnp.log(total)


def attend_call(q, k, v, bias, rows):
    ext, width = q.shape
    blocks = rows // BLK
    return pl.pallas_call(
        attend_kernel,
        grid=(blocks,),
        in_specs=[
            const_spec((ext, width)),
            const_spec((ext, width)),
            const_spec((ext, width)),
            pl.BlockSpec((1, 2 * BLK, BLK), lambda i: (i, 0, 0)),
        ],
        out_specs=[row_spec(BLK, width), pl.BlockSpec((1, 8, 2 * BLK), lambda i: (i, 0, 0))],
        out_shape=[
            jax.ShapeDtypeStruct((rows, width), bf16),
            jax.ShapeDtypeStruct((blocks, 8, 2 * BLK), f32),
        ],
        compiler_params=params(32),
        cost_estimate=SMALL,
        name="attend",
    )(q, k, v, bias)


def mlp_kernel(
    x_ref,
    og_ref,
    attn_ref,
    gain_ref,
    wa_ref,
    wi_ref,
    wo_ref,
    out_ref,
    gmid_ref,
    lowmid_ref,
    dattn_ref,
    low2_ref,
    act_ref,
    ggu_ref,
    gain_grad_ref,
):
    gain = gain_ref[...]
    middle = x_ref[...].astype(f32) + nn(attn_ref[...], wa_ref[...])
    normed, inv = row_stats(middle)
    low_two = (normed * gain).astype(bf16)
    low2_ref[...] = low_two
    og = og_ref[...]
    ff = wo_ref.shape[0]
    chunk = 384
    result = middle
    grad_n = jnp.zeros(middle.shape, f32)
    for c in range(ff // chunk):
        sl = slice(c * chunk, c * chunk + chunk)
        gate = nt(low_two, wi_ref[0, sl])
        up = nt(low_two, wi_ref[1, sl])
        wo = wo_ref[sl]
        phi = 0.5 + 0.5 * lax.erf(gate * (0.5**0.5))
        gel = gate * phi
        act = (gel * up).astype(bf16)
        act_ref[:, sl] = act
        result = result + nn(act, wo)
        grad_act = nt(og, wo)
        dens = jnp.exp(-0.5 * gate * gate) * 0.3989422804014327
        g_gate = (grad_act * up * (phi + gate * dens)).astype(bf16)
        g_up = (grad_act * gel).astype(bf16)
        ggu_ref[:, sl] = g_gate
        ggu_ref[:, ff + c * chunk : ff + c * chunk + chunk] = g_up
        grad_n = grad_n + nn(g_gate, wi_ref[0, sl]) + nn(g_up, wi_ref[1, sl])
    out_ref[...] = result.astype(bf16)

    @pl.when(pl.program_id(0) == 0)
    def _():
        gain_grad_ref[...] = jnp.zeros(gain_grad_ref.shape, f32)

    gain_grad_ref[...] += fold_rows(grad_n * normed)
    u = grad_n * gain
    grad_mid = og.astype(f32) + inv * (
        u
        - jnp.mean(u, axis=-1, keepdims=True)
        - normed * jnp.mean(u * normed, axis=-1, keepdims=True)
    )
    gmid_ref[...] = grad_mid
    low_mid = grad_mid.astype(bf16)
    lowmid_ref[...] = low_mid
    dattn_ref[...] = nt(low_mid, wa_ref[...]).astype(bf16)


def mlp_call(x, og, attn, gain, wa, wi, wo):
    rows, width = x.shape
    ff = wo.shape[0]
    blk = 256
    low = jax.ShapeDtypeStruct((rows, width), bf16)
    return pl.pallas_call(
        mlp_kernel,
        grid=(rows // blk,),
        in_specs=[row_spec(blk, width)] * 3
        + [const_spec((1, width)), const_spec(wa.shape), const_spec(wi.shape), const_spec(wo.shape)],
        out_specs=[row_spec(blk, width)] * 5
        + [row_spec(blk, ff), row_spec(blk, 2 * ff), pl.BlockSpec((8, width), lambda i: (0, 0))],
        out_shape=[
            low,
            jax.ShapeDtypeStruct((rows, width), f32),
            low,
            low,
            low,
            jax.ShapeDtypeStruct((rows, ff), bf16),
            jax.ShapeDtypeStruct((rows, 2 * ff), bf16),
            jax.ShapeDtypeStruct((8, width), f32),
        ],
        compiler_params=params(48),
        cost_estimate=SMALL,
        name="mlp",
    )(x, og, attn, gain, wa, wi, wo)


def attend_back_kernel(
    first_pair,
    q_ref,
    k_ref,
    v_ref,
    do_ref,
    bias_ref,
    lse_ref,
    cos_ref,
    sin_ref,
    dq_ref,
    dk_out_ref,
    dv_out_ref,
    dk_ref,
    dv_ref,
):
    b = pl.program_id(0)
    start = pl.multiple_of(b * BLK, BLK)

    @pl.when(b == 0)
    def _():
        dk_ref[...] = jnp.zeros(dk_ref.shape, f32)
        dv_ref[...] = jnp.zeros(dv_ref.shape, f32)

    bias = bias_ref[0]
    bias = jnp.concatenate([bias, bias], axis=1)
    rows = pl.ds(start, 2 * BLK)
    cos = cos_ref[pl.ds(start + HALF, BLK), :] * 0.125
    sin = sin_ref[pl.ds(start + HALF, BLK), :] * 0.125
    for j in range(q_ref.shape[1] // 128):
        cols = slice(128 * j, 128 * j + 128)
        qs = stack_pair(q_ref[pl.ds(start + HALF, BLK), cols], 0.125)
        dos = stack_pair(do_ref[:, cols], 1.0)
        kb = k_ref[rows, cols]
        vb = v_ref[rows, cols]
        p = jnp.exp(nt(kb, qs) + bias - lse_ref[0, first_pair + j : first_pair + j + 1, :])
        dp = nt(vb, dos)
        dot = jnp.sum(p * dp, axis=0, keepdims=True)
        ds = (p * (dp - dot)).astype(bf16)
        dv_ref[rows, cols] += nn(p.astype(bf16), dos)
        dk_ref[rows, cols] += nn(ds, qs)
        dq = merge_pair(tn(ds, kb))
        dq_ref[:, cols] = (dq * cos + turn_lanes(dq * sin, 1.0)).astype(bf16)

    @pl.when(b == pl.num_programs(0) - 1)
    def _():
        dk_out_ref[...] = dk_ref[...].astype(bf16)
        dv_out_ref[...] = dv_ref[...].astype(bf16)


def attend_back_call(q, k, v, do, bias, lse, cos, sin, at, width):
    ext = q.shape[0]
    rows = do.shape[0]
    full = pl.BlockSpec((ext, width), lambda i: (0, at), pipeline_mode=pl.Buffered(1))
    acc = pl.BlockSpec((ext, width), lambda i: (0, 0))
    return pl.pallas_call(
        functools.partial(attend_back_kernel, at * (width // 128)),
        grid=(rows // BLK,),
        in_specs=[
            full,
            full,
            full,
            pl.BlockSpec((BLK, width), lambda i: (i, at)),
            pl.BlockSpec((1, 2 * BLK, BLK), lambda i: (i, 0, 0)),
            pl.BlockSpec((1, 8, 2 * BLK), lambda i: (i, 0, 0)),
            const_spec((ext, 128)),
            const_spec((ext, 128)),
        ],
        out_specs=[
            row_spec(BLK, width),
            acc,
            acc,
        ],
        out_shape=[
            jax.ShapeDtypeStruct((rows, width), bf16),
            jax.ShapeDtypeStruct((ext, width), bf16),
            jax.ShapeDtypeStruct((ext, width), bf16),
        ],
        scratch_shapes=[pltpu.VMEM((ext, width), f32)] * 2,
        compiler_params=params(48),
        cost_estimate=SMALL,
        name="attend_back",
    )(q, k, v, do, bias, lse, cos, sin)


def mixed_kernel(first_ref, last_ref, cos_ref, sin_ref, *refs):
    mix_ref = refs[-1]
    rows = mix_ref.shape[0]
    width = mix_ref.shape[1] // 3
    i = pl.program_id(0)
    own = pl.ds(pl.multiple_of(i * rows, rows) + HALF, rows)
    is_first = (i == 0).astype(f32)
    is_last = (i == pl.num_programs(0) - 1).astype(f32)
    at = 0
    for n in range(len(refs) // 3):
        dq_ref, dk_ref, dv_ref = refs[3 * n : 3 * n + 3]
        part = dq_ref.shape[1]
        pad = jnp.zeros((rows - HALF, part), f32)
        cos = jnp.concatenate([cos_ref[own, :]] * (part // 128), axis=1)
        sin = jnp.concatenate([sin_ref[own, :]] * (part // 128), axis=1)

        def joined(ref, start):
            cols = slice(start, start + part)
            head = first_ref[:, cols].astype(f32) * is_first
            tail = last_ref[:, cols].astype(f32) * is_last
            ends = jnp.concatenate([head, pad], axis=0) + jnp.concatenate([pad, tail], axis=0)
            return ref[own, :].astype(f32) + ends

        mix_ref[:, at : at + part] = dq_ref[...]
        dk = joined(dk_ref, at)
        dk = (dk * cos + turn_lanes(dk * sin, 1.0)).astype(bf16)
        mix_ref[:, width + at : width + at + part] = dk
        dv = joined(dv_ref, width + at)
        mix_ref[:, 2 * width + at : 2 * width + at + part] = dv.astype(bf16)
        at += part


def mixed_call(pieces, first, last, cos, sin):
    rows = pieces[0][0].shape[0]
    width = sum(piece[0].shape[1] for piece in pieces)
    blk = 256
    specs = []
    for dq, dk, dv in pieces:
        specs += [row_spec(blk, dq.shape[1]), const_spec(dk.shape), const_spec(dv.shape)]
    return pl.pallas_call(
        mixed_kernel,
        grid=(rows // blk,),
        in_specs=[const_spec(x.shape) for x in (first, last, cos, sin)] + specs,
        out_specs=row_spec(blk, 3 * width),
        out_shape=jax.ShapeDtypeStruct((rows, 3 * width), bf16),
        compiler_params=params(32),
        cost_estimate=SMALL,
        name="mixed",
    )(first, last, cos, sin, *[x for piece in pieces for x in piece])


def input_grad_kernel(mix_ref, w_ref, x_ref, gmid_ref, gain_ref, out_ref, gain_grad_ref):
    grad_n = nn(mix_ref[...], w_ref[...])
    normed, inv = row_stats(x_ref[...].astype(f32))

    @pl.when(pl.program_id(0) == 0)
    def _():
        gain_grad_ref[...] = jnp.zeros(gain_grad_ref.shape, f32)

    gain_grad_ref[...] += fold_rows(grad_n * normed)
    u = grad_n * gain_ref[...]
    out_ref[...] = (
        gmid_ref[...]
        + inv
        * (
            u
            - jnp.mean(u, axis=-1, keepdims=True)
            - normed * jnp.mean(u * normed, axis=-1, keepdims=True)
        )
    ).astype(bf16)


def input_grad_call(mix, w, x, gmid, gain):
    rows, width = x.shape
    blk = 256
    return pl.pallas_call(
        input_grad_kernel,
        grid=(rows // blk,),
        in_specs=[
            row_spec(blk, 3 * width),
            const_spec(w.shape),
            row_spec(blk, width),
            row_spec(blk, width),
            const_spec((1, width)),
        ],
        out_specs=[row_spec(blk, width), pl.BlockSpec((8, width), lambda i: (0, 0))],
        out_shape=[
            jax.ShapeDtypeStruct((rows, width), bf16),
            jax.ShapeDtypeStruct((8, width), f32),
        ],
        compiler_params=params(40),
        cost_estimate=SMALL,
        name="input_grad",
    )(mix, w, x, gmid, gain)


def dp_swap(x, mask):
    count = lax.axis_size("dp")
    return lax.ppermute(x, "dp", [(i, i ^ mask) for i in range(count)])


def ring_shift(x, step):
    count = lax.axis_size("tensor")
    return lax.ppermute(x, "tensor", [(i, (i + step) % count) for i in range(count)])


def pair_swap(x):
    count = lax.axis_size("tensor")
    return lax.ppermute(x, "tensor", [(i, i ^ 1) for i in range(count)])


def index_dim(x, at, dim):
    return lax.squeeze(lax.dynamic_slice_in_dim(x, at, 1, dim), (dim,))


def core_rows(x, core, dim):
    rows = x.shape[dim]
    size = (rows // 2 + 7) // 8 * 8
    step = (rows - size) // 8
    tiles = x.reshape(x.shape[:dim] + (rows // 8, 8) + x.shape[dim + 1 :])
    part = lax.dynamic_slice_in_dim(tiles, core * step, size // 8, dim)
    return part.reshape(x.shape[:dim] + (size,) + x.shape[dim + 1 :])


def join_cores(a, b, rows, dim):
    size = a.shape[dim]
    keep = rows - size
    return jnp.concatenate([a, lax.slice_in_dim(b, size - keep, size, axis=dim)], axis=dim)


def hold(value, *after):
    return lax.optimization_barrier((value,) + after)[0]


def spread_quads(piece):
    half = (piece.shape[1] // 2 + 7) // 8 * 8
    from_x = dp_swap(piece, XBIT)
    from_y = dp_swap(piece, YBIT)
    return piece, from_x, from_y, half


def spread_diag(piece, from_x, from_y, half):
    diag_x = dp_swap(from_y[:, :half], XBIT)
    diag_y = dp_swap(from_x[:, half:], YBIT)
    early = dp_swap(jnp.stack([piece, from_x, from_y]), CORE)
    return early, diag_x, diag_y


def spread_core(piece, from_x, from_y, early, diag_x, diag_y):
    diag = jnp.concatenate([diag_x, diag_y], axis=1)
    late = dp_swap(diag, CORE)
    return [piece, from_x, from_y, diag], [early[0], early[1], early[2], late]


def spread_all(piece, *after):
    mine = jnp.stack([piece] + [dp_swap(piece, mask) for mask in (XBIT, YBIT, XBIT | YBIT)])
    theirs = dp_swap(hold(mine, *after), CORE)
    return mine, theirs


def ring_pieces(piece):
    return jnp.stack([ring_shift(piece, s) for s in range(1, lax.axis_size("tensor"))])


def by_core(mine, theirs, core):
    first = core == 0
    return jnp.where(first, mine, theirs), jnp.where(first, theirs, mine)


def add(a, b):
    return (a.astype(f32) + b.astype(f32)).astype(bf16)


def halve(arr, at, mask, dim):
    got = dp_swap(index_dim(arr, 1 - at, dim), mask)
    return index_dim(arr, at, dim), got


def reduce_first(total, quad):
    steps, _, rows, width = total.shape
    grid = total.reshape(steps, 2, 2, rows, width)
    half = steps // 2
    return halve(grid[:half], quad & 1, XBIT, 2) + halve(grid[half:], quad >> 1, YBIT, 1)


def reduce_second(keep_x, got_x, keep_y, got_y, quad):
    first = add(keep_x, got_x)
    second = add(keep_y, got_y)
    return halve(first, quad >> 1, YBIT, 1) + halve(second, quad & 1, XBIT, 1)


def reduce_ring(keep_y, got_y, keep_x, got_x, extra=None):
    first = add(keep_y, got_y)
    second = add(keep_x, got_x)
    half = first.shape[0]
    steps = half + second.shape[0]
    parts = [first[s] for s in range(half)] + [second[s] for s in range(steps - half)]
    mask = 8
    if lax.axis_size("dp") > mask:
        block = jnp.stack(parts)
        while mask < lax.axis_size("dp"):
            block = add(block, dp_swap(block, mask))
            mask *= 2
        parts = [block[s] for s in range(steps)]
    if extra is not None:
        parts = [jnp.concatenate([part, extra]) for part in parts]
    return [parts[0]] + [ring_shift(parts[s], -s) for s in range(1, steps)]


def reduce_sum(parts):
    result = parts[0].astype(f32)
    for part in parts[1:]:
        result = result + part.astype(f32)
    return result.astype(bf16)


def put(buf, part, starts):
    return lax.dynamic_update_slice(buf, part, starts)


def tables(seg_ids, first_row, rows):
    count = seg_ids.shape[0]
    places = jnp.arange(count, dtype=jnp.int32)
    earlier = jnp.concatenate([jnp.full((1,), -1, jnp.int32), seg_ids[:-1]])
    starts = jnp.where(seg_ids != earlier, places, 0)
    positions = places - lax.cummax(starts, axis=0)
    ext = rows + WINDOW
    seg_ext = lax.dynamic_slice(jnp.pad(seg_ids, HALF, constant_values=-1), (first_row,), (ext,))
    pos_ext = lax.dynamic_slice(jnp.pad(positions, HALF), (first_row,), (ext,))
    freq = ROPE_BASE ** (-jnp.arange(0, 64, 2).astype(f32) / 64)
    angles = pos_ext.astype(f32)[:, None] * jnp.concatenate([freq] * 4)[None, :]
    blocks = rows // BLK
    seg_rows = seg_ext.reshape(blocks + 1, BLK)
    seg_k = jnp.concatenate([seg_rows[:-1], seg_rows[1:]], axis=1)
    seg_q = seg_ext[HALF : HALF + rows].reshape(blocks, BLK)
    k_place = jnp.arange(2 * BLK, dtype=jnp.int32)[:, None] - HALF
    q_place = jnp.arange(BLK, dtype=jnp.int32)[None, :]
    near = jnp.abs(k_place - q_place) <= HALF
    allowed = near[None] & (seg_k[:, :, None] == seg_q[:, None, :])
    bias = jnp.where(allowed, 0.0, -1e30).astype(f32)
    return jnp.cos(angles), jnp.sin(angles), bias


def body(
    hidden_in,
    seg_ids,
    norm1_gain,
    norm2_gain,
    qkv_weight,
    attn_weight,
    mlp_in_weight,
    mlp_out_weight,
    out_grad,
):
    rows, width = hidden_in.shape
    steps = lax.axis_size("tensor")
    here = lax.axis_index("tensor")
    at_dp = lax.axis_index("dp")
    core = at_dp & 1
    quad = (at_dp >> 1) & 3
    odd = (here & 1) == 1
    w_qkv = qkv_weight.transpose(1, 2, 3, 0).reshape(3, 4, 48, width)
    w_in = mlp_in_weight.transpose(1, 2, 0).reshape(2, 4, 72, width)
    w_out = mlp_out_weight.reshape(4, 72, width)
    w_attn = attn_weight.reshape(4, 48, width)

    own_qkv = core_rows(index_dim(w_qkv, quad, 1), core, 1).reshape(3 * 24, width)
    ring_qkv = ring_pieces(own_qkv)
    x_held = hold(hidden_in, ring_qkv)
    edge = jnp.where(odd, x_held[:HALF], x_held[-HALF:])
    halo = pair_swap(edge)
    none = jnp.zeros_like(halo)
    x_ext = jnp.concatenate(
        [jnp.where(odd, halo, none), x_held, jnp.where(odd, none, halo)], axis=0
    )

    quads_qkv = spread_quads(ring_qkv)
    diag_qkv = spread_diag(*quads_qkv)
    wi_held = hold(w_in, quads_qkv[1], quads_qkv[2])
    wo_held = hold(w_out, quads_qkv[1], quads_qkv[2])
    wa_held = hold(w_attn, quads_qkv[1], quads_qkv[2])
    own_rest = jnp.concatenate(
        [
            index_dim(index_dim(wi_held, core, 0), quad, 0),
            core_rows(index_dim(wo_held, quad, 0), core, 0),
            core_rows(index_dim(wa_held, quad, 0), core, 0),
        ],
        axis=0,
    )
    ring_rest = ring_pieces(own_rest)
    quads_rest = spread_quads(ring_rest)
    mine, theirs = spread_core(*quads_qkv[:3], *diag_qkv)
    qkv_all = jnp.zeros((3, steps, 4, 48, width), bf16)
    qkv_all = qkv_all.at[:, 0].set(hold(w_qkv, quads_qkv[1], quads_qkv[2]))
    for n in range(4):
        a, b = by_core(mine[n], theirs[n], core)
        a = a.reshape(steps - 1, 3, 24, width)
        b = b.reshape(steps - 1, 3, 24, width)
        part = join_cores(a, b, 48, 2).transpose(1, 0, 2, 3)[:, :, None]
        qkv_all = put(qkv_all, part, (0, 1, quad ^ n, 0, 0))
    qkv_all = qkv_all.reshape(3, width, width)

    cos, sin, bias = tables(hold(seg_ids, ring_qkv), here * rows, rows)
    gain_one = norm1_gain[None]
    gain_two = norm2_gain[None]
    low_one, q, k, v = qkv_call(x_ext, gain_one, hold(qkv_all, ring_rest), cos, sin)
    low_attn, lse = attend_call(q, k, v, bias, rows)

    piece, from_x, from_y, half = quads_rest
    early, diag_x, diag_y = spread_diag(piece, hold(from_x, q), hold(from_y, q), half)
    mine, theirs = spread_core(piece, from_x, from_y, early, hold(diag_x, low_attn), diag_y)
    wi_held = hold(w_in, q)
    wo_held = hold(w_out, q)
    wa_held = hold(w_attn, q)
    in_all = jnp.zeros((2, steps, 4, 72, width), bf16).at[:, 0].set(wi_held)
    out_all = jnp.zeros((steps, 4, 72, width), bf16).at[0].set(wo_held)
    attn_all = jnp.zeros((steps, 4, 48, width), bf16).at[0].set(wa_held)
    for n in range(4):
        a, b = by_core(mine[n], theirs[n], core)
        pair = jnp.stack([a[:, :72], b[:, :72]])[:, :, None]
        in_all = put(in_all, pair, (0, 1, quad ^ n, 0, 0))
        out_all = put(
            out_all, join_cores(a[:, 72:112], b[:, 72:112], 72, 1)[:, None], (1, quad ^ n, 0, 0)
        )
        attn_all = put(
            attn_all, join_cores(a[:, 112:], b[:, 112:], 48, 1)[:, None], (1, quad ^ n, 0, 0)
        )
    ff = steps * 288
    in_all = in_all.reshape(2, ff, width)
    out_all = out_all.reshape(ff, width)
    attn_all = attn_all.reshape(width, width)

    result, grad_mid, low_mid, dattn, low_two, low_act, ggu, gain_two_part = mlp_call(
        hidden_in, out_grad, low_attn, gain_two, attn_all, in_all, out_all
    )

    def halves(x):
        cols = width // 2
        return [lax.dynamic_slice_in_dim(x, c * cols, cols, 1) for c in (1 - core, core)]

    def grads(x, ys, *lead):
        shape = lead + (steps, 4, x.shape[1] // (4 * steps * lead[0] if lead else 4 * steps))
        return [tn(x, y).astype(bf16).reshape(shape + (width // 2,)) for y in ys]

    g_in = grads(ggu, halves(low_two), 2)
    g_out = grads(low_act, halves(out_grad))
    g_attn = grads(low_attn, halves(low_mid))
    got_in = dp_swap(g_in[0], CORE)
    got_out = dp_swap(g_out[0], CORE)
    got_attn = dp_swap(g_attn[0], CORE)
    dattn = hold(dattn, *g_in, *g_out, *g_attn)
    piece_a = attend_back_call(q, k, v, dattn, bias, lse, cos, sin, 2, 256)
    sum_in = add(g_in[1], hold(got_in, piece_a[0]))
    core_rest = jnp.concatenate(
        [sum_in[0], sum_in[1], add(g_out[1], got_out), add(g_attn[1], got_attn)], axis=2
    )
    first_rest = reduce_first(core_rest, quad)
    dattn = hold(dattn, core_rest, piece_a[0])
    piece_b = attend_back_call(q, k, v, dattn, bias, lse, cos, sin, 0, 384)
    dattn = hold(dattn, *first_rest[1::2], piece_b[0])
    piece_c = attend_back_call(q, k, v, dattn, bias, lse, cos, sin, 3, 128)
    second_rest = reduce_second(*first_rest, quad)
    pieces = (piece_b, piece_c, piece_a)
    ends = [
        jnp.concatenate([jnp.where(odd, x[:HALF], x[-HALF:]) for x in (p[n] for p in pieces)], axis=1)
        for n in (1, 2)
    ]
    got = pair_swap(jnp.stack(ends, axis=1))
    turn = width // steps
    got = jnp.where(odd, jnp.roll(got, turn, 2), jnp.roll(got, -turn, 2)).reshape(HALF, 2 * width)
    none = jnp.zeros_like(got)
    own = slice(HALF, HALF + rows)
    mix = mixed_call(pieces, jnp.where(odd, got, none), jnp.where(odd, none, got), cos, sin)
    g_qkv = [
        tn(mix, y).astype(bf16).reshape(3, steps, 4, 48, width // 2)
        for y in halves(low_one[HALF : HALF + rows])
    ]
    got_qkv = dp_swap(g_qkv[0], CORE)
    core_qkv = add(g_qkv[1], got_qkv).transpose(1, 2, 0, 3, 4).reshape(steps, 4, 144, width // 2)
    first_qkv = reduce_first(core_qkv, quad)
    ring_back = reduce_ring(*second_rest)
    grad_hidden, gain_one_part = input_grad_call(
        hold(mix, core_qkv, *second_rest[1::2]),
        qkv_all.reshape(3 * width, width),
        hidden_in,
        grad_mid,
        gain_one,
    )
    gains = jnp.stack([jnp.sum(gain_one_part, axis=0), jnp.sum(gain_two_part, axis=0)])
    mask = 8
    while mask < lax.axis_size("dp"):
        gains = gains + dp_swap(gains, mask)
        mask *= 2

    def coded(x):
        high = lax.reduce_precision(x, 8, 7)
        return jnp.concatenate([high, x - high]).astype(bf16).reshape(8, width // 2)

    def decoded(x):
        both = x.astype(f32).reshape(x.shape[:-2] + (2, 2, width))
        return both[..., 0, :, :] + both[..., 1, :, :]

    second_qkv = reduce_second(*first_qkv, quad)
    parts = reduce_ring(*second_qkv, coded(gains))
    slots = jnp.zeros((steps, 8, width // 2), bf16)
    for s in range(steps):
        slots = put(slots, parts[s][None, 144:], ((here + s) % steps if s else here, 0, 0))
    gains = jnp.sum(decoded(slots), axis=0)
    rest = reduce_sum(ring_back)
    qkv_total = reduce_sum([part[:144] for part in parts])

    mine, theirs = spread_all(jnp.concatenate([rest, qkv_total, coded(gains)]))
    full = jnp.where(
        core == 0,
        jnp.concatenate([mine, theirs], axis=2),
        jnp.concatenate([theirs, mine], axis=2),
    )
    o_in = jnp.zeros((2, 4, 72, width), f32)
    o_out = jnp.zeros((4, 72, width), f32)
    o_attn = jnp.zeros((4, 48, width), f32)
    o_qkv = jnp.zeros((3, 4, 48, width), f32)
    slots = jnp.zeros((4, 8, width), bf16)
    for n in range(4):
        a = full[n]
        slots = put(slots, a[None, 408:], (quad ^ n, 0, 0))
        a = a[:408].astype(f32)
        o_in = put(o_in, a[:144].reshape(2, 1, 72, width), (0, quad ^ n, 0, 0))
        o_out = put(o_out, a[None, 144:216], (quad ^ n, 0, 0))
        o_attn = put(o_attn, a[None, 216:264], (quad ^ n, 0, 0))
        o_qkv = put(o_qkv, a[264:].reshape(3, 1, 48, width), (0, quad ^ n, 0, 0))
    cols = width // 2
    gains = jnp.sum(decoded(slots[..., :cols]), axis=0) + jnp.sum(decoded(slots[..., cols:]), axis=0)
    grad_qkv = o_qkv.reshape(3, 3, 64, width).transpose(3, 0, 1, 2)
    grad_in = o_in.reshape(2, 288, width).transpose(2, 0, 1)
    return (
        result,
        grad_hidden,
        gains[0],
        gains[1],
        grad_qkv,
        o_attn.reshape(192, width),
        grad_in,
        o_out.reshape(288, width),
    )


def solution(mesh):
    rows = P(("dp", "tensor"), None)
    in_specs = (
        rows,
        P("dp"),
        P(),
        P(),
        P(None, None, "tensor", None),
        P("tensor", None),
        P(None, None, "tensor"),
        P("tensor", None),
        rows,
    )
    out_specs = (
        rows,
        rows,
        P(),
        P(),
        P(None, None, "tensor", None),
        P("tensor", None),
        P(None, None, "tensor"),
        P("tensor", None),
    )
    return jax.shard_map(body, mesh=mesh, in_specs=in_specs, out_specs=out_specs, check_vma=False)
```

```python
import functools

import jax
import jax.numpy as jnp
from jax import lax
from jax.experimental import pallas as pl
from jax.experimental.pallas import tpu as pltpu
from jax.sharding import PartitionSpec as P

WINDOW = 128
HALF = WINDOW // 2
EPS = 1e-05
ROPE_BASE = 10000.0
BLK = 128
CORE, XBIT, YBIT = 1, 2, 4
bf16 = jnp.bfloat16
f32 = jnp.float32
MIB = 1024 * 1024
SMALL = pl.CostEstimate(flops=1000, bytes_accessed=1000, transcendentals=0)


def nn(a, b):
    return lax.dot_general(a, b, (((1,), (0,)), ((), ())), preferred_element_type=f32)


def nt(a, b):
    return lax.dot_general(a, b, (((1,), (1,)), ((), ())), preferred_element_type=f32)


def tn(a, b):
    return lax.dot_general(a, b, (((0,), (0,)), ((), ())), preferred_element_type=f32)


def row_stats(x):
    mean = jnp.mean(x, axis=-1, keepdims=True)
    cen = x - mean
    inv = lax.rsqrt(jnp.mean(cen * cen, axis=-1, keepdims=True) + EPS)
    return cen * inv, inv


def fold_rows(x):
    return jnp.sum(x.reshape(x.shape[0] // 8, 8, x.shape[1]), axis=0)


def const_spec(shape):
    zeros = (0,) * len(shape)
    return pl.BlockSpec(shape, lambda i: zeros, pipeline_mode=pl.Buffered(1))


def row_spec(rows, cols):
    return pl.BlockSpec((rows, cols), lambda i: (i, 0))


def flag_spec():
    return pl.BlockSpec(memory_space=pltpu.SMEM)


def core_halves(x, core):
    cols = x.shape[1] // 2
    left, right = x[:, :cols], x[:, cols:]
    first = (jnp.zeros((1, cols), jnp.int32) + core) == 0
    return jnp.where(first, right, left).astype(bf16), jnp.where(first, left, right).astype(bf16)


def params(mib):
    return pltpu.CompilerParams(
        dimension_semantics=("arbitrary",), vmem_limit_bytes=mib * MIB
    )


def turn_lanes(z, lo_sign):
    width = z.shape[1]
    lane = lax.broadcasted_iota(jnp.int32, (1, width), 1)
    first = lane % 64 < 32
    ahead = pltpu.roll(z, width - 32, 1)
    behind = pltpu.roll(z, 32, 1)
    return jnp.where(first, lo_sign * ahead, -lo_sign * behind)


def qkv_kernel(x_ref, gain_ref, w_ref, cos_ref, sin_ref, q_ref, k_ref, v_ref):
    normed, _ = row_stats(x_ref[...].astype(f32))
    low = (normed * gain_ref[...]).astype(bf16)
    width = low.shape[1]
    cos = jnp.concatenate([cos_ref[...]] * (width // 128), axis=1)
    sin = jnp.concatenate([sin_ref[...]] * (width // 128), axis=1)
    q = nt(low, w_ref[0])
    q_ref[...] = (q * cos + turn_lanes(q, -1.0) * sin).astype(bf16)
    k = nt(low, w_ref[1])
    k_ref[...] = (k * cos + turn_lanes(k, -1.0) * sin).astype(bf16)
    v_ref[...] = nt(low, w_ref[2]).astype(bf16)


def qkv_call(x_ext, gain, w, cos, sin):
    rows, width = x_ext.shape
    blk = rows // 3
    out = jax.ShapeDtypeStruct((rows, width), bf16)
    return pl.pallas_call(
        qkv_kernel,
        grid=(rows // blk,),
        in_specs=[
            row_spec(blk, width),
            const_spec((1, width)),
            const_spec(w.shape),
            row_spec(blk, 128),
            row_spec(blk, 128),
        ],
        out_specs=[row_spec(blk, width)] * 3,
        out_shape=[out] * 3,
        compiler_params=params(40),
        cost_estimate=SMALL,
        name="qkv",
    )(x_ext, gain, w, cos, sin)


def stack_pair(z, scale):
    lane = lax.broadcasted_iota(jnp.int32, (1, 128), 1)
    low_head = (lane < 64).astype(f32) * scale
    high_head = (lane >= 64).astype(f32) * scale
    return jnp.concatenate([z * low_head.astype(bf16), z * high_head.astype(bf16)], axis=0)


def merge_pair(z):
    rows = z.shape[0] // 2
    lane = lax.broadcasted_iota(jnp.int32, (1, 128), 1)
    return jnp.where(lane < 64, z[:rows], z[rows:])


def attend_kernel(q_ref, k_ref, v_ref, bias_ref, out_ref, lse_ref):
    b = pl.program_id(0)
    start = pl.multiple_of(b * BLK, BLK)
    bias = bias_ref[0]
    bias = jnp.concatenate([bias, bias], axis=1)
    for j in range(q_ref.shape[1] // 128):
        cols = slice(128 * j, 128 * j + 128)
        qs = stack_pair(q_ref[pl.ds(start + HALF, BLK), cols], 0.125)
        kb = k_ref[pl.ds(start, 2 * BLK), cols]
        vb = v_ref[pl.ds(start, 2 * BLK), cols]
        s = nt(kb, qs) + bias
        top = jnp.max(s, axis=0, keepdims=True)
        e = jnp.exp(s - top)
        total = jnp.sum(e, axis=0, keepdims=True)
        low_p = (e * (1.0 / total)).astype(bf16)
        out_ref[:, cols] = merge_pair(tn(low_p, vb)).astype(bf16)
        lse_ref[0, j : j + 1, :] = top + jnp.log(total)


def attend_call(q, k, v, bias, rows):
    ext, width = q.shape
    blocks = rows // BLK
    return pl.pallas_call(
        attend_kernel,
        grid=(blocks,),
        in_specs=[
            const_spec((ext, width)),
            const_spec((ext, width)),
            const_spec((ext, width)),
            pl.BlockSpec((1, 2 * BLK, BLK), lambda i: (i, 0, 0)),
        ],
        out_specs=[row_spec(BLK, width), pl.BlockSpec((1, 8, 2 * BLK), lambda i: (i, 0, 0))],
        out_shape=[
            jax.ShapeDtypeStruct((rows, width), bf16),
            jax.ShapeDtypeStruct((blocks, 8, 2 * BLK), f32),
        ],
        compiler_params=params(32),
        cost_estimate=SMALL,
        name="attend",
    )(q, k, v, bias)


def mlp_kernel(
    core_ref,
    x_ref,
    og_ref,
    attn_ref,
    gain_ref,
    wa_ref,
    wi_ref,
    wo_ref,
    out_ref,
    gmid_ref,
    dattn_ref,
    mid_send_ref,
    mid_keep_ref,
    two_send_ref,
    two_keep_ref,
    og_send_ref,
    og_keep_ref,
    act_ref,
    ggu_ref,
    gain_grad_ref,
):
    core = core_ref[0]
    gain = gain_ref[...]
    middle = x_ref[...].astype(f32) + nn(attn_ref[...], wa_ref[...])
    normed, inv = row_stats(middle)
    low_two = (normed * gain).astype(bf16)
    two_send_ref[...], two_keep_ref[...] = core_halves(normed * gain, core)
    og = og_ref[...]
    og_send_ref[...], og_keep_ref[...] = core_halves(og.astype(f32), core)
    ff = wo_ref.shape[0]
    chunk = 384
    result = middle
    grad_n = jnp.zeros(middle.shape, f32)
    for c in range(ff // chunk):
        sl = slice(c * chunk, c * chunk + chunk)
        gate = nt(low_two, wi_ref[0, sl])
        up = nt(low_two, wi_ref[1, sl])
        wo = wo_ref[sl]
        phi = 0.5 + 0.5 * lax.erf(gate * (0.5**0.5))
        gel = gate * phi
        act = (gel * up).astype(bf16)
        act_ref[:, sl] = act
        result = result + nn(act, wo)
        grad_act = nt(og, wo)
        dens = jnp.exp(-0.5 * gate * gate) * 0.3989422804014327
        g_gate = (grad_act * up * (phi + gate * dens)).astype(bf16)
        g_up = (grad_act * gel).astype(bf16)
        ggu_ref[:, sl] = g_gate
        ggu_ref[:, ff + c * chunk : ff + c * chunk + chunk] = g_up
        grad_n = grad_n + nn(g_gate, wi_ref[0, sl]) + nn(g_up, wi_ref[1, sl])
    out_ref[...] = result.astype(bf16)

    @pl.when(pl.program_id(0) == 0)
    def _():
        gain_grad_ref[...] = jnp.zeros(gain_grad_ref.shape, f32)

    gain_grad_ref[...] += fold_rows(grad_n * normed)
    u = grad_n * gain
    grad_mid = og.astype(f32) + inv * (
        u
        - jnp.mean(u, axis=-1, keepdims=True)
        - normed * jnp.mean(u * normed, axis=-1, keepdims=True)
    )
    gmid_ref[...] = grad_mid
    low_mid = grad_mid.astype(bf16)
    mid_send_ref[...], mid_keep_ref[...] = core_halves(grad_mid, core)
    dattn_ref[...] = nt(low_mid, wa_ref[...]).astype(bf16)


def mlp_call(core, x, og, attn, gain, wa, wi, wo):
    rows, width = x.shape
    ff = wo.shape[0]
    blk = 512
    low = jax.ShapeDtypeStruct((rows, width), bf16)
    return pl.pallas_call(
        mlp_kernel,
        grid=(rows // blk,),
        in_specs=[flag_spec()]
        + [row_spec(blk, width)] * 3
        + [const_spec((1, width)), const_spec(wa.shape), const_spec(wi.shape), const_spec(wo.shape)],
        out_specs=[row_spec(blk, width)] * 3
        + [row_spec(blk, width // 2)] * 6
        + [row_spec(blk, ff), row_spec(blk, 2 * ff), pl.BlockSpec((8, width), lambda i: (0, 0))],
        out_shape=[low, jax.ShapeDtypeStruct((rows, width), f32), low]
        + [jax.ShapeDtypeStruct((rows, width // 2), bf16)] * 6
        + [
            jax.ShapeDtypeStruct((rows, ff), bf16),
            jax.ShapeDtypeStruct((rows, 2 * ff), bf16),
            jax.ShapeDtypeStruct((8, width), f32),
        ],
        compiler_params=params(48),
        cost_estimate=SMALL,
        name="mlp",
    )(core, x, og, attn, gain, wa, wi, wo)


def attend_back_kernel(
    first_pair,
    q_ref,
    k_ref,
    v_ref,
    do_ref,
    bias_ref,
    lse_ref,
    cos_ref,
    sin_ref,
    dq_ref,
    dk_out_ref,
    dv_out_ref,
    dk_ref,
    dv_ref,
):
    b = pl.program_id(0)
    start = pl.multiple_of(b * BLK, BLK)

    @pl.when(b == 0)
    def _():
        dk_ref[...] = jnp.zeros(dk_ref.shape, f32)
        dv_ref[...] = jnp.zeros(dv_ref.shape, f32)

    bias = bias_ref[0]
    bias = jnp.concatenate([bias, bias], axis=1)
    rows = pl.ds(start, 2 * BLK)
    cos = cos_ref[pl.ds(start + HALF, BLK), :] * 0.125
    sin = sin_ref[pl.ds(start + HALF, BLK), :] * 0.125
    for j in range(q_ref.shape[1] // 128):
        cols = slice(128 * j, 128 * j + 128)
        qs = stack_pair(q_ref[pl.ds(start + HALF, BLK), cols], 0.125)
        dos = stack_pair(do_ref[:, cols], 1.0)
        kb = k_ref[rows, cols]
        vb = v_ref[rows, cols]
        p = jnp.exp(nt(kb, qs) + bias - lse_ref[0, first_pair + j : first_pair + j + 1, :])
        dp = nt(vb, dos)
        dot = jnp.sum(p * dp, axis=0, keepdims=True)
        ds = (p * (dp - dot)).astype(bf16)
        dv_ref[rows, cols] += nn(p.astype(bf16), dos)
        dk_ref[rows, cols] += nn(ds, qs)
        dq = merge_pair(tn(ds, kb))
        dq_ref[:, cols] = (dq * cos + turn_lanes(dq * sin, 1.0)).astype(bf16)

    @pl.when(b == pl.num_programs(0) - 1)
    def _():
        dk_out_ref[...] = dk_ref[...].astype(bf16)
        dv_out_ref[...] = dv_ref[...].astype(bf16)


def attend_back_call(q, k, v, do, bias, lse, cos, sin, at, width):
    ext = q.shape[0]
    rows = do.shape[0]
    full = pl.BlockSpec((ext, width), lambda i: (0, at), pipeline_mode=pl.Buffered(1))
    acc = pl.BlockSpec((ext, width), lambda i: (0, 0))
    return pl.pallas_call(
        functools.partial(attend_back_kernel, at * (width // 128)),
        grid=(rows // BLK,),
        in_specs=[
            full,
            full,
            full,
            pl.BlockSpec((BLK, width), lambda i: (i, at)),
            pl.BlockSpec((1, 2 * BLK, BLK), lambda i: (i, 0, 0)),
            pl.BlockSpec((1, 8, 2 * BLK), lambda i: (i, 0, 0)),
            const_spec((ext, 128)),
            const_spec((ext, 128)),
        ],
        out_specs=[
            row_spec(BLK, width),
            acc,
            acc,
        ],
        out_shape=[
            jax.ShapeDtypeStruct((rows, width), bf16),
            jax.ShapeDtypeStruct((ext, width), bf16),
            jax.ShapeDtypeStruct((ext, width), bf16),
        ],
        scratch_shapes=[pltpu.VMEM((ext, width), f32)] * 2,
        compiler_params=params(48),
        cost_estimate=SMALL,
        name="attend_back",
    )(q, k, v, do, bias, lse, cos, sin)


def mixed_kernel(core_ref, x_ref, gain_ref, first_ref, last_ref, cos_ref, sin_ref, *refs):
    mix_ref, send_ref, keep_ref = refs[-3:]
    normed, _ = row_stats(x_ref[...].astype(f32))
    send_ref[...], keep_ref[...] = core_halves(normed * gain_ref[...], core_ref[0])
    rows = mix_ref.shape[0]
    width = mix_ref.shape[1] // 3
    i = pl.program_id(0)
    own = pl.ds(pl.multiple_of(i * rows, rows) + HALF, rows)
    is_first = (i == 0).astype(f32)
    is_last = (i == pl.num_programs(0) - 1).astype(f32)
    at = 0
    for n in range(len(refs) // 3 - 1):
        dq_ref, dk_ref, dv_ref = refs[3 * n : 3 * n + 3]
        part = dq_ref.shape[1]
        pad = jnp.zeros((rows - HALF, part), f32)
        cos = jnp.concatenate([cos_ref[own, :]] * (part // 128), axis=1)
        sin = jnp.concatenate([sin_ref[own, :]] * (part // 128), axis=1)

        def joined(ref, start):
            cols = slice(start, start + part)
            head = first_ref[:, cols].astype(f32) * is_first
            tail = last_ref[:, cols].astype(f32) * is_last
            ends = jnp.concatenate([head, pad], axis=0) + jnp.concatenate([pad, tail], axis=0)
            return ref[own, :].astype(f32) + ends

        mix_ref[:, at : at + part] = dq_ref[...]
        dk = joined(dk_ref, at)
        dk = (dk * cos + turn_lanes(dk * sin, 1.0)).astype(bf16)
        mix_ref[:, width + at : width + at + part] = dk
        dv = joined(dv_ref, width + at)
        mix_ref[:, 2 * width + at : 2 * width + at + part] = dv.astype(bf16)
        at += part


def mixed_call(core, x, gain, pieces, first, last, cos, sin):
    rows = x.shape[0]
    width = sum(piece[0].shape[1] for piece in pieces)
    blk = 256
    specs = []
    for dq, dk, dv in pieces:
        specs += [row_spec(blk, dq.shape[1]), const_spec(dk.shape), const_spec(dv.shape)]
    return pl.pallas_call(
        mixed_kernel,
        grid=(rows // blk,),
        in_specs=[flag_spec(), row_spec(blk, width), const_spec(gain.shape)]
        + [const_spec(y.shape) for y in (first, last, cos, sin)]
        + specs,
        out_specs=[row_spec(blk, 3 * width)] + [row_spec(blk, width // 2)] * 2,
        out_shape=[jax.ShapeDtypeStruct((rows, 3 * width), bf16)]
        + [jax.ShapeDtypeStruct((rows, width // 2), bf16)] * 2,
        compiler_params=params(32),
        cost_estimate=SMALL,
        name="mixed",
    )(core, x, gain, first, last, cos, sin, *[y for piece in pieces for y in piece])


def input_grad_kernel(mix_ref, w_ref, x_ref, gmid_ref, gain_ref, *refs):
    out_ref, gain_grad_ref = refs[-2:]
    grad_n = nn(mix_ref[...], w_ref[...])
    normed, inv = row_stats(x_ref[...].astype(f32))

    @pl.when(pl.program_id(0) == 0)
    def _():
        gain_grad_ref[...] = jnp.zeros(gain_grad_ref.shape, f32)

    gain_grad_ref[...] += fold_rows(grad_n * normed)
    u = grad_n * gain_ref[...]
    out_ref[...] = (
        gmid_ref[...]
        + inv
        * (
            u
            - jnp.mean(u, axis=-1, keepdims=True)
            - normed * jnp.mean(u * normed, axis=-1, keepdims=True)
        )
    ).astype(bf16)


def input_grad_call(mix, w, x, gmid, gain, after):
    rows, width = x.shape
    blk = 256
    return pl.pallas_call(
        input_grad_kernel,
        grid=(rows // blk,),
        in_specs=[
            row_spec(blk, 3 * width),
            const_spec(w.shape),
            row_spec(blk, width),
            row_spec(blk, width),
            const_spec((1, width)),
        ]
        + [pl.BlockSpec(memory_space=pl.ANY)] * len(after),
        out_specs=[row_spec(blk, width), pl.BlockSpec((8, width), lambda i: (0, 0))],
        out_shape=[
            jax.ShapeDtypeStruct((rows, width), bf16),
            jax.ShapeDtypeStruct((8, width), f32),
        ],
        compiler_params=params(40),
        cost_estimate=SMALL,
        name="input_grad",
    )(mix, w, x, gmid, gain, *after)


def assemble_kernel(place_ref, mine_ref, theirs_ref, in_ref, out_ref, attn_ref, qkv_ref, gain_ref):
    a = mine_ref[0].astype(f32)
    b = theirs_ref[0].astype(f32)
    cols = a.shape[1]
    first = (jnp.zeros((1, cols), jnp.int32) + place_ref[0]) == 0
    for part, at in ((jnp.where(first, a, b), 0), (jnp.where(first, b, a), cols)):
        sl = slice(at, at + cols)
        in_ref[0, 0, :, sl] = part[:72]
        in_ref[1, 0, :, sl] = part[72:144]
        out_ref[0, :, sl] = part[144:216]
        attn_ref[0, :, sl] = part[216:264]
        for c in range(3):
            qkv_ref[c, 0, :, sl] = part[264 + 48 * c : 312 + 48 * c]
        gain_ref[0, :, sl] = part[408:]


def assemble_call(place, mine, theirs):
    width = 2 * mine.shape[2]
    block = pl.BlockSpec((1,) + mine.shape[1:], lambda n, place: (n, 0, 0))
    flat = lambda n, place: (place[1] ^ n, 0, 0)
    deep = lambda n, place: (0, place[1] ^ n, 0, 0)
    shapes = [(2, 4, 72, width), (4, 72, width), (4, 48, width), (3, 4, 48, width), (4, 8, width)]
    return pl.pallas_call(
        assemble_kernel,
        grid_spec=pltpu.PrefetchScalarGridSpec(
            num_scalar_prefetch=1,
            grid=(4,),
            in_specs=[block, block],
            out_specs=[
                pl.BlockSpec((2, 1, 72, width), deep),
                pl.BlockSpec((1, 72, width), flat),
                pl.BlockSpec((1, 48, width), flat),
                pl.BlockSpec((3, 1, 48, width), deep),
                pl.BlockSpec((1, 8, width), flat),
            ],
        ),
        out_shape=[jax.ShapeDtypeStruct(shape, f32) for shape in shapes],
        compiler_params=params(32),
        cost_estimate=SMALL,
        name="assemble",
    )(place, mine, theirs)


def dp_swap(x, mask):
    count = lax.axis_size("dp")
    return lax.ppermute(x, "dp", [(i, i ^ mask) for i in range(count)])


def ring_shift(x, step):
    count = lax.axis_size("tensor")
    return lax.ppermute(x, "tensor", [(i, (i + step) % count) for i in range(count)])


def pair_swap(x):
    count = lax.axis_size("tensor")
    return lax.ppermute(x, "tensor", [(i, i ^ 1) for i in range(count)])


def index_dim(x, at, dim):
    return lax.squeeze(lax.dynamic_slice_in_dim(x, at, 1, dim), (dim,))


def core_rows(x, core, dim):
    rows = x.shape[dim]
    size = (rows // 2 + 7) // 8 * 8
    step = (rows - size) // 8
    tiles = x.reshape(x.shape[:dim] + (rows // 8, 8) + x.shape[dim + 1 :])
    part = lax.dynamic_slice_in_dim(tiles, core * step, size // 8, dim)
    return part.reshape(x.shape[:dim] + (size,) + x.shape[dim + 1 :])


def join_cores(a, b, rows, dim):
    size = a.shape[dim]
    keep = rows - size
    return jnp.concatenate([a, lax.slice_in_dim(b, size - keep, size, axis=dim)], axis=dim)


def hold(value, *after):
    return lax.optimization_barrier((value,) + after)[0]


def spread_quads(piece):
    half = (piece.shape[1] // 2 + 7) // 8 * 8
    from_x = dp_swap(piece, XBIT)
    from_y = dp_swap(piece, YBIT)
    return piece, from_x, from_y, half


def spread_diag(piece, from_x, from_y, half):
    diag_x = dp_swap(from_y[:, :half], XBIT)
    diag_y = dp_swap(from_x[:, half:], YBIT)
    early = dp_swap(jnp.stack([piece, from_x, from_y]), CORE)
    return early, diag_x, diag_y


def spread_core(piece, from_x, from_y, early, diag_x, diag_y):
    diag = jnp.concatenate([diag_x, diag_y], axis=1)
    late = dp_swap(diag, CORE)
    return [piece, from_x, from_y, diag], [early[0], early[1], early[2], late]


def spread_all(piece, *after):
    mine = jnp.stack([piece] + [dp_swap(piece, mask) for mask in (XBIT, YBIT, XBIT | YBIT)])
    theirs = dp_swap(hold(mine, *after), CORE)
    return mine, theirs


def ring_pieces(piece):
    return jnp.stack([ring_shift(piece, s) for s in range(1, lax.axis_size("tensor"))])


def by_core(mine, theirs, core):
    first = core == 0
    return jnp.where(first, mine, theirs), jnp.where(first, theirs, mine)


def add(a, b):
    return (a.astype(f32) + b.astype(f32)).astype(bf16)


def halve(arr, at, mask, dim):
    send = index_dim(arr, 1 - at, dim)
    return index_dim(arr, at, dim), dp_swap(send, mask), send


def reduce_first(total, quad):
    steps, _, rows, width = total.shape
    grid = total.reshape(steps, 2, 2, rows, width)
    half = steps // 2
    keep_x, got_x, send_x = halve(grid[:half], quad & 1, XBIT, 2)
    keep_y, got_y, send_y = halve(grid[half:], quad >> 1, YBIT, 1)
    return (keep_x, got_x, keep_y, got_y), (send_x, send_y)


def reduce_second(keep_x, got_x, keep_y, got_y, quad):
    first = add(keep_x, got_x)
    second = add(keep_y, got_y)
    keep_y, got_y, send_y = halve(first, quad >> 1, YBIT, 1)
    keep_x, got_x, send_x = halve(second, quad & 1, XBIT, 1)
    return (keep_y, got_y, keep_x, got_x), (send_y, send_x)


def reduce_ring(keep_y, got_y, keep_x, got_x, extra=None):
    first = add(keep_y, got_y)
    second = add(keep_x, got_x)
    half = first.shape[0]
    steps = half + second.shape[0]
    parts = [first[s] for s in range(half)] + [second[s] for s in range(steps - half)]
    mask = 8
    if lax.axis_size("dp") > mask:
        block = jnp.stack(parts)
        while mask < lax.axis_size("dp"):
            block = add(block, dp_swap(block, mask))
            mask *= 2
        parts = [block[s] for s in range(steps)]
    if extra is not None:
        parts = [jnp.concatenate([part, extra]) for part in parts]
    return [parts[0]] + [ring_shift(parts[s], -s) for s in range(1, steps)], parts[1:]


def reduce_sum(parts):
    result = parts[0].astype(f32)
    for part in parts[1:]:
        result = result + part.astype(f32)
    return result.astype(bf16)


def put(buf, part, starts):
    return lax.dynamic_update_slice(buf, part, starts)


def tables(seg_ids, first_row, rows):
    count = seg_ids.shape[0]
    places = jnp.arange(count, dtype=jnp.int32)
    earlier = jnp.concatenate([jnp.full((1,), -1, jnp.int32), seg_ids[:-1]])
    starts = jnp.where(seg_ids != earlier, places, 0)
    positions = places - lax.cummax(starts, axis=0)
    ext = rows + WINDOW
    seg_ext = lax.dynamic_slice(jnp.pad(seg_ids, HALF, constant_values=-1), (first_row,), (ext,))
    pos_ext = lax.dynamic_slice(jnp.pad(positions, HALF), (first_row,), (ext,))
    freq = ROPE_BASE ** (-jnp.arange(0, 64, 2).astype(f32) / 64)
    angles = pos_ext.astype(f32)[:, None] * jnp.concatenate([freq] * 4)[None, :]
    blocks = rows // BLK
    seg_rows = seg_ext.reshape(blocks + 1, BLK)
    seg_k = jnp.concatenate([seg_rows[:-1], seg_rows[1:]], axis=1)
    seg_q = seg_ext[HALF : HALF + rows].reshape(blocks, BLK)
    k_place = jnp.arange(2 * BLK, dtype=jnp.int32)[:, None] - HALF
    q_place = jnp.arange(BLK, dtype=jnp.int32)[None, :]
    near = jnp.abs(k_place - q_place) <= HALF
    allowed = near[None] & (seg_k[:, :, None] == seg_q[:, None, :])
    bias = jnp.where(allowed, 0.0, -1e30).astype(f32)
    return jnp.cos(angles), jnp.sin(angles), bias, pos_ext


def body(
    hidden_in,
    seg_ids,
    norm1_gain,
    norm2_gain,
    qkv_weight,
    attn_weight,
    mlp_in_weight,
    mlp_out_weight,
    out_grad,
):
    rows, width = hidden_in.shape
    steps = lax.axis_size("tensor")
    here = lax.axis_index("tensor")
    at_dp = lax.axis_index("dp")
    core = at_dp & 1
    quad = (at_dp >> 1) & 3
    odd = (here & 1) == 1
    w_qkv = qkv_weight.transpose(1, 2, 3, 0).reshape(3, 4, 48, width)
    w_in = mlp_in_weight.transpose(1, 2, 0).reshape(2, 4, 72, width)
    w_out = mlp_out_weight.reshape(4, 72, width)
    w_attn = attn_weight.reshape(4, 48, width)

    own_qkv = core_rows(index_dim(w_qkv, quad, 1), core, 1).reshape(3 * 24, width)
    ring_qkv = ring_pieces(own_qkv)
    x_held = hold(hidden_in, ring_qkv)
    edge = jnp.where(odd, x_held[:HALF], x_held[-HALF:])
    halo = pair_swap(edge)
    none = jnp.zeros_like(halo)
    x_ext = jnp.concatenate(
        [jnp.where(odd, halo, none), x_held, jnp.where(odd, none, halo)], axis=0
    )

    cos, sin, bias, pos_ext = tables(hold(seg_ids, ring_qkv), here * rows, rows)
    quads_qkv = spread_quads(ring_qkv)
    diag_qkv = spread_diag(*quads_qkv)
    wi_held = hold(w_in, pos_ext)
    wo_held = hold(w_out, pos_ext)
    wa_held = hold(w_attn, pos_ext)
    own_rest = jnp.concatenate(
        [
            index_dim(index_dim(wi_held, core, 0), quad, 0),
            core_rows(index_dim(wo_held, quad, 0), core, 0),
            core_rows(index_dim(wa_held, quad, 0), core, 0),
        ],
        axis=0,
    )
    ring_rest = ring_pieces(own_rest)
    quads_rest = spread_quads(ring_rest)
    mine, theirs = spread_core(*quads_qkv[:3], *diag_qkv)
    qkv_all = jnp.zeros((3, steps, 4, 48, width), bf16)
    qkv_all = qkv_all.at[:, 0].set(hold(w_qkv, quads_qkv[1], quads_qkv[2]))
    for n in range(4):
        a, b = by_core(mine[n], theirs[n], core)
        a = a.reshape(steps - 1, 3, 24, width)
        b = b.reshape(steps - 1, 3, 24, width)
        part = join_cores(a, b, 48, 2).transpose(1, 0, 2, 3)[:, :, None]
        qkv_all = put(qkv_all, part, (0, 1, quad ^ n, 0, 0))
    qkv_all = qkv_all.reshape(3, width, width)

    gain_one = norm1_gain[None]
    gain_two = norm2_gain[None]
    q, k, v = qkv_call(x_ext, gain_one, hold(qkv_all, ring_rest), cos, sin)
    low_attn, lse = attend_call(q, k, v, bias, rows)

    piece, from_x, from_y, half = quads_rest
    early, diag_x, diag_y = spread_diag(piece, hold(from_x, q), hold(from_y, q), half)
    mine, theirs = spread_core(piece, from_x, from_y, early, hold(diag_x, low_attn), diag_y)
    wi_held = hold(w_in, q)
    wo_held = hold(w_out, q)
    wa_held = hold(w_attn, q)
    in_all = jnp.zeros((2, steps, 4, 72, width), bf16).at[:, 0].set(wi_held)
    out_all = jnp.zeros((steps, 4, 72, width), bf16).at[0].set(wo_held)
    attn_all = jnp.zeros((steps, 4, 48, width), bf16).at[0].set(wa_held)
    for n in range(4):
        a, b = by_core(mine[n], theirs[n], core)
        pair = jnp.stack([a[:, :72], b[:, :72]])[:, :, None]
        in_all = put(in_all, pair, (0, 1, quad ^ n, 0, 0))
        out_all = put(
            out_all, join_cores(a[:, 72:112], b[:, 72:112], 72, 1)[:, None], (1, quad ^ n, 0, 0)
        )
        attn_all = put(
            attn_all, join_cores(a[:, 112:], b[:, 112:], 48, 1)[:, None], (1, quad ^ n, 0, 0)
        )
    ff = steps * 288
    in_all = in_all.reshape(2, ff, width)
    out_all = out_all.reshape(ff, width)
    attn_all = attn_all.reshape(width, width)

    core_flag = core.astype(jnp.int32)[None]
    (
        result,
        grad_mid,
        dattn,
        mid_send,
        mid_keep,
        two_send,
        two_keep,
        og_send,
        og_keep,
        low_act,
        ggu,
        gain_two_part,
    ) = mlp_call(
        core_flag, hidden_in, out_grad, low_attn, gain_two, attn_all, in_all, out_all
    )

    def grads(x, ys, *lead):
        shape = lead + (steps, 4, x.shape[1] // (4 * steps * lead[0] if lead else 4 * steps))
        return [tn(x, y).astype(bf16).reshape(shape + (width // 2,)) for y in ys]

    g_in = grads(ggu, (two_send, two_keep), 2)
    g_out = grads(low_act, (og_send, og_keep))
    g_attn = grads(low_attn, (mid_send, mid_keep))
    got_in = dp_swap(g_in[0], CORE)
    got_out = dp_swap(g_out[0], CORE)
    got_attn = dp_swap(g_attn[0], CORE)
    dattn = hold(dattn, *g_in, *g_out, *g_attn)
    piece_a = attend_back_call(q, k, v, dattn, bias, lse, cos, sin, 2, 256)
    sum_in = add(g_in[1], hold(got_in, piece_a[0]))
    core_rest = jnp.concatenate(
        [sum_in[0], sum_in[1], add(g_out[1], got_out), add(g_attn[1], got_attn)], axis=2
    )
    first_rest, _ = reduce_first(core_rest, quad)
    dattn = hold(dattn, core_rest, piece_a[0])
    piece_b = attend_back_call(q, k, v, dattn, bias, lse, cos, sin, 0, 384)
    dattn = hold(dattn, *first_rest[1::2], piece_b[0])
    piece_c = attend_back_call(q, k, v, dattn, bias, lse, cos, sin, 3, 128)
    second_rest, _ = reduce_second(*first_rest, quad)
    pieces = (piece_b, piece_c, piece_a)
    ends = [
        jnp.concatenate([jnp.where(odd, x[:HALF], x[-HALF:]) for x in (p[n] for p in pieces)], axis=1)
        for n in (1, 2)
    ]
    got = pair_swap(jnp.stack(ends, axis=1))
    turn = width // steps
    got = jnp.where(odd, jnp.roll(got, turn, 2), jnp.roll(got, -turn, 2)).reshape(HALF, 2 * width)
    none = jnp.zeros_like(got)
    own = slice(HALF, HALF + rows)
    mix, one_send, one_keep = mixed_call(
        core_flag,
        hidden_in,
        gain_one,
        pieces,
        jnp.where(odd, got, none),
        jnp.where(odd, none, got),
        cos,
        sin,
    )
    g_qkv = [
        tn(mix, y).astype(bf16).reshape(3, steps, 4, 48, width // 2)
        for y in (one_send, one_keep)
    ]
    got_qkv = dp_swap(g_qkv[0], CORE)
    core_qkv = add(g_qkv[1], got_qkv).transpose(1, 2, 0, 3, 4).reshape(steps, 4, 144, width // 2)
    first_qkv, sent_qkv = reduce_first(core_qkv, quad)
    ring_back, sent_rest = reduce_ring(*second_rest)
    grad_hidden, gain_one_part = input_grad_call(
        mix,
        qkv_all.reshape(3 * width, width),
        hidden_in,
        grad_mid,
        gain_one,
        (*sent_qkv, *sent_rest),
    )
    gains = jnp.stack([jnp.sum(gain_one_part, axis=0), jnp.sum(gain_two_part, axis=0)])
    mask = 8
    while mask < lax.axis_size("dp"):
        gains = gains + dp_swap(gains, mask)
        mask *= 2

    def coded(x):
        high = lax.reduce_precision(x, 8, 7)
        return jnp.concatenate([high, x - high]).astype(bf16).reshape(8, width // 2)

    def decoded(x):
        both = x.astype(f32).reshape(x.shape[:-2] + (2, 2, width))
        return both[..., 0, :, :] + both[..., 1, :, :]

    second_qkv, _ = reduce_second(*first_qkv, quad)
    parts, _ = reduce_ring(*second_qkv, coded(gains))
    slots = jnp.zeros((steps, 8, width // 2), bf16)
    for s in range(steps):
        slots = put(slots, parts[s][None, 144:], ((here + s) % steps if s else here, 0, 0))
    gains = jnp.sum(decoded(slots), axis=0)
    rest = reduce_sum(ring_back)
    qkv_total = reduce_sum([part[:144] for part in parts])

    mine, theirs = spread_all(jnp.concatenate([rest, qkv_total, coded(gains)]))
    place = jnp.stack([core, quad]).astype(jnp.int32)
    o_in, o_out, o_attn, o_qkv, slots = assemble_call(place, mine, theirs)
    slots = slots.reshape(4, 8, 2, width // 2).transpose(0, 2, 1, 3)
    gains = jnp.sum(decoded(slots.reshape(8, 8, width // 2)), axis=0)
    grad_qkv = o_qkv.reshape(3, 3, 64, width).transpose(3, 0, 1, 2)
    grad_in = o_in.reshape(2, 288, width).transpose(2, 0, 1)
    return (
        result,
        grad_hidden,
        gains[0],
        gains[1],
        grad_qkv,
        o_attn.reshape(192, width),
        grad_in,
        o_out.reshape(288, width),
    )


def solution(mesh):
    rows = P(("dp", "tensor"), None)
    in_specs = (
        rows,
        P("dp"),
        P(),
        P(),
        P(None, None, "tensor", None),
        P("tensor", None),
        P(None, None, "tensor"),
        P("tensor", None),
        rows,
    )
    out_specs = (
        rows,
        rows,
        P(),
        P(),
        P(None, None, "tensor", None),
        P("tensor", None),
        P(None, None, "tensor"),
        P("tensor", None),
    )
    return jax.shard_map(body, mesh=mesh, in_specs=in_specs, out_specs=out_specs, check_vma=False)
```

```python
import functools

import jax
import jax.numpy as jnp
from jax import lax
from jax.experimental import pallas as pl
from jax.experimental.pallas import tpu as pltpu
from jax.sharding import PartitionSpec as P

WINDOW = 128
HALF = WINDOW // 2
EPS = 1e-05
ROPE_BASE = 10000.0
BLK = 128
CORE, XBIT, YBIT = 1, 2, 4
bf16 = jnp.bfloat16
f32 = jnp.float32
MIB = 1024 * 1024
SMALL = pl.CostEstimate(flops=1000, bytes_accessed=1000, transcendentals=0)


def nn(a, b):
    return lax.dot_general(a, b, (((1,), (0,)), ((), ())), preferred_element_type=f32)


def nt(a, b):
    return lax.dot_general(a, b, (((1,), (1,)), ((), ())), preferred_element_type=f32)


def tn(a, b):
    return lax.dot_general(a, b, (((0,), (0,)), ((), ())), preferred_element_type=f32)


def row_stats(x):
    mean = jnp.mean(x, axis=-1, keepdims=True)
    cen = x - mean
    inv = lax.rsqrt(jnp.mean(cen * cen, axis=-1, keepdims=True) + EPS)
    return cen * inv, inv


def fold_rows(x):
    return jnp.sum(x.reshape(x.shape[0] // 8, 8, x.shape[1]), axis=0)


def const_spec(shape):
    zeros = (0,) * len(shape)
    return pl.BlockSpec(shape, lambda i: zeros, pipeline_mode=pl.Buffered(1))


def row_spec(rows, cols):
    return pl.BlockSpec((rows, cols), lambda i: (i, 0))


def flag_spec():
    return pl.BlockSpec(memory_space=pltpu.SMEM)


def core_halves(x, core):
    cols = x.shape[1] // 2
    left, right = x[:, :cols], x[:, cols:]
    first = (jnp.zeros((1, cols), jnp.int32) + core) == 0
    return jnp.where(first, right, left).astype(bf16), jnp.where(first, left, right).astype(bf16)


def params(mib):
    return pltpu.CompilerParams(
        dimension_semantics=("arbitrary",), vmem_limit_bytes=mib * MIB
    )


def turn_lanes(z, lo_sign):
    width = z.shape[1]
    lane = lax.broadcasted_iota(jnp.int32, (1, width), 1)
    first = lane % 64 < 32
    ahead = pltpu.roll(z, width - 32, 1)
    behind = pltpu.roll(z, 32, 1)
    return jnp.where(first, lo_sign * ahead, -lo_sign * behind)


def qkv_kernel(x_ref, gain_ref, w_ref, cos_ref, sin_ref, q_ref, k_ref, v_ref):
    normed, _ = row_stats(x_ref[...].astype(f32))
    low = (normed * gain_ref[...]).astype(bf16)
    width = low.shape[1]
    cos = jnp.concatenate([cos_ref[...]] * (width // 128), axis=1)
    sin = jnp.concatenate([sin_ref[...]] * (width // 128), axis=1)
    q = nt(low, w_ref[0])
    q_ref[...] = (q * cos + turn_lanes(q, -1.0) * sin).astype(bf16)
    k = nt(low, w_ref[1])
    k_ref[...] = (k * cos + turn_lanes(k, -1.0) * sin).astype(bf16)
    v_ref[...] = nt(low, w_ref[2]).astype(bf16)


def qkv_call(x_ext, gain, w, cos, sin):
    rows, width = x_ext.shape
    blk = rows // 3
    out = jax.ShapeDtypeStruct((rows, width), bf16)
    return pl.pallas_call(
        qkv_kernel,
        grid=(rows // blk,),
        in_specs=[
            row_spec(blk, width),
            const_spec((1, width)),
            const_spec(w.shape),
            row_spec(blk, 128),
            row_spec(blk, 128),
        ],
        out_specs=[row_spec(blk, width)] * 3,
        out_shape=[out] * 3,
        compiler_params=params(40),
        cost_estimate=SMALL,
        name="qkv",
    )(x_ext, gain, w, cos, sin)


def stack_pair(z, scale):
    lane = lax.broadcasted_iota(jnp.int32, (1, 128), 1)
    low_head = (lane < 64).astype(f32) * scale
    high_head = (lane >= 64).astype(f32) * scale
    return jnp.concatenate([z * low_head.astype(bf16), z * high_head.astype(bf16)], axis=0)


def merge_pair(z):
    rows = z.shape[0] // 2
    lane = lax.broadcasted_iota(jnp.int32, (1, 128), 1)
    return jnp.where(lane < 64, z[:rows], z[rows:])


def attend_kernel(q_ref, k_ref, v_ref, bias_ref, out_ref, lse_ref):
    b = pl.program_id(0)
    start = pl.multiple_of(b * BLK, BLK)
    bias = bias_ref[0]
    bias = jnp.concatenate([bias, bias], axis=1)
    for j in range(q_ref.shape[1] // 128):
        cols = slice(128 * j, 128 * j + 128)
        qs = stack_pair(q_ref[pl.ds(start + HALF, BLK), cols], 0.125)
        kb = k_ref[pl.ds(start, 2 * BLK), cols]
        vb = v_ref[pl.ds(start, 2 * BLK), cols]
        s = nt(kb, qs) + bias
        top = jnp.max(s, axis=0, keepdims=True)
        e = jnp.exp(s - top)
        total = jnp.sum(e, axis=0, keepdims=True)
        low_p = (e * (1.0 / total)).astype(bf16)
        out_ref[:, cols] = merge_pair(tn(low_p, vb)).astype(bf16)
        lse_ref[0, j : j + 1, :] = top + jnp.log(total)


def attend_call(q, k, v, bias, rows):
    ext, width = q.shape
    blocks = rows // BLK
    return pl.pallas_call(
        attend_kernel,
        grid=(blocks,),
        in_specs=[
            const_spec((ext, width)),
            const_spec((ext, width)),
            const_spec((ext, width)),
            pl.BlockSpec((1, 2 * BLK, BLK), lambda i: (i, 0, 0)),
        ],
        out_specs=[row_spec(BLK, width), pl.BlockSpec((1, 8, 2 * BLK), lambda i: (i, 0, 0))],
        out_shape=[
            jax.ShapeDtypeStruct((rows, width), bf16),
            jax.ShapeDtypeStruct((blocks, 8, 2 * BLK), f32),
        ],
        compiler_params=params(32),
        cost_estimate=SMALL,
        name="attend",
    )(q, k, v, bias)


def mlp_kernel(
    core_ref,
    x_ref,
    og_ref,
    attn_ref,
    gain_ref,
    wa_ref,
    wi_ref,
    wo_ref,
    out_ref,
    gmid_ref,
    dattn_ref,
    mid_send_ref,
    mid_keep_ref,
    two_send_ref,
    two_keep_ref,
    og_send_ref,
    og_keep_ref,
    act_ref,
    ggu_ref,
    gain_grad_ref,
):
    core = core_ref[0]
    gain = gain_ref[...]
    middle = x_ref[...].astype(f32) + nn(attn_ref[...], wa_ref[...])
    normed, inv = row_stats(middle)
    low_two = (normed * gain).astype(bf16)
    two_send_ref[...], two_keep_ref[...] = core_halves(normed * gain, core)
    og = og_ref[...]
    og_send_ref[...], og_keep_ref[...] = core_halves(og.astype(f32), core)
    ff = wo_ref.shape[0]
    chunk = 384
    result = middle
    grad_n = jnp.zeros(middle.shape, f32)
    for c in range(ff // chunk):
        sl = slice(c * chunk, c * chunk + chunk)
        gate = nt(low_two, wi_ref[0, sl])
        up = nt(low_two, wi_ref[1, sl])
        wo = wo_ref[sl]
        phi = 0.5 + 0.5 * lax.erf(gate * (0.5**0.5))
        gel = gate * phi
        act = (gel * up).astype(bf16)
        act_ref[:, sl] = act
        result = result + nn(act, wo)
        grad_act = nt(og, wo)
        dens = jnp.exp(-0.5 * gate * gate) * 0.3989422804014327
        g_gate = (grad_act * up * (phi + gate * dens)).astype(bf16)
        g_up = (grad_act * gel).astype(bf16)
        ggu_ref[:, sl] = g_gate
        ggu_ref[:, ff + c * chunk : ff + c * chunk + chunk] = g_up
        grad_n = grad_n + nn(g_gate, wi_ref[0, sl]) + nn(g_up, wi_ref[1, sl])
    out_ref[...] = result.astype(bf16)

    @pl.when(pl.program_id(0) == 0)
    def _():
        gain_grad_ref[...] = jnp.zeros(gain_grad_ref.shape, f32)

    gain_grad_ref[...] += fold_rows(grad_n * normed)
    u = grad_n * gain
    grad_mid = og.astype(f32) + inv * (
        u
        - jnp.mean(u, axis=-1, keepdims=True)
        - normed * jnp.mean(u * normed, axis=-1, keepdims=True)
    )
    gmid_ref[...] = grad_mid
    low_mid = grad_mid.astype(bf16)
    mid_send_ref[...], mid_keep_ref[...] = core_halves(grad_mid, core)
    dattn_ref[...] = nt(low_mid, wa_ref[...]).astype(bf16)


def mlp_call(core, x, og, attn, gain, wa, wi, wo):
    rows, width = x.shape
    ff = wo.shape[0]
    blk = 512
    low = jax.ShapeDtypeStruct((rows, width), bf16)
    return pl.pallas_call(
        mlp_kernel,
        grid=(rows // blk,),
        in_specs=[flag_spec()]
        + [row_spec(blk, width)] * 3
        + [const_spec((1, width)), const_spec(wa.shape), const_spec(wi.shape), const_spec(wo.shape)],
        out_specs=[row_spec(blk, width)] * 3
        + [row_spec(blk, width // 2)] * 6
        + [row_spec(blk, ff), row_spec(blk, 2 * ff), pl.BlockSpec((8, width), lambda i: (0, 0))],
        out_shape=[low, jax.ShapeDtypeStruct((rows, width), f32), low]
        + [jax.ShapeDtypeStruct((rows, width // 2), bf16)] * 6
        + [
            jax.ShapeDtypeStruct((rows, ff), bf16),
            jax.ShapeDtypeStruct((rows, 2 * ff), bf16),
            jax.ShapeDtypeStruct((8, width), f32),
        ],
        compiler_params=params(48),
        cost_estimate=SMALL,
        name="mlp",
    )(core, x, og, attn, gain, wa, wi, wo)


def attend_back_kernel(
    first_pair,
    q_ref,
    k_ref,
    v_ref,
    do_ref,
    bias_ref,
    lse_ref,
    cos_ref,
    sin_ref,
    dq_ref,
    dk_out_ref,
    dv_out_ref,
    dk_ref,
    dv_ref,
):
    b = pl.program_id(0)
    start = pl.multiple_of(b * BLK, BLK)

    @pl.when(b == 0)
    def _():
        dk_ref[...] = jnp.zeros(dk_ref.shape, f32)
        dv_ref[...] = jnp.zeros(dv_ref.shape, f32)

    bias = bias_ref[0]
    bias = jnp.concatenate([bias, bias], axis=1)
    rows = pl.ds(start, 2 * BLK)
    cos = cos_ref[pl.ds(start + HALF, BLK), :] * 0.125
    sin = sin_ref[pl.ds(start + HALF, BLK), :] * 0.125
    for j in range(q_ref.shape[1] // 128):
        cols = slice(128 * j, 128 * j + 128)
        qs = stack_pair(q_ref[pl.ds(start + HALF, BLK), cols], 0.125)
        dos = stack_pair(do_ref[:, cols], 1.0)
        kb = k_ref[rows, cols]
        vb = v_ref[rows, cols]
        p = jnp.exp(nt(kb, qs) + bias - lse_ref[0, first_pair + j : first_pair + j + 1, :])
        dp = nt(vb, dos)
        dot = jnp.sum(p * dp, axis=0, keepdims=True)
        ds = (p * (dp - dot)).astype(bf16)
        dv_ref[rows, cols] += nn(p.astype(bf16), dos)
        dk_ref[rows, cols] += nn(ds, qs)
        dq = merge_pair(tn(ds, kb))
        dq_ref[:, cols] = (dq * cos + turn_lanes(dq * sin, 1.0)).astype(bf16)

    @pl.when(b == pl.num_programs(0) - 1)
    def _():
        dk_out_ref[...] = dk_ref[...].astype(bf16)
        dv_out_ref[...] = dv_ref[...].astype(bf16)


def attend_back_call(q, k, v, do, bias, lse, cos, sin, at, width):
    ext = q.shape[0]
    rows = do.shape[0]
    full = pl.BlockSpec((ext, width), lambda i: (0, at), pipeline_mode=pl.Buffered(1))
    acc = pl.BlockSpec((ext, width), lambda i: (0, 0))
    return pl.pallas_call(
        functools.partial(attend_back_kernel, at * (width // 128)),
        grid=(rows // BLK,),
        in_specs=[
            full,
            full,
            full,
            pl.BlockSpec((BLK, width), lambda i: (i, at)),
            pl.BlockSpec((1, 2 * BLK, BLK), lambda i: (i, 0, 0)),
            pl.BlockSpec((1, 8, 2 * BLK), lambda i: (i, 0, 0)),
            const_spec((ext, 128)),
            const_spec((ext, 128)),
        ],
        out_specs=[
            row_spec(BLK, width),
            acc,
            acc,
        ],
        out_shape=[
            jax.ShapeDtypeStruct((rows, width), bf16),
            jax.ShapeDtypeStruct((ext, width), bf16),
            jax.ShapeDtypeStruct((ext, width), bf16),
        ],
        scratch_shapes=[pltpu.VMEM((ext, width), f32)] * 2,
        compiler_params=params(48),
        cost_estimate=SMALL,
        name="attend_back",
    )(q, k, v, do, bias, lse, cos, sin)


def mixed_kernel(core_ref, x_ref, gain_ref, first_ref, last_ref, cos_ref, sin_ref, *refs):
    mix_ref, send_ref, keep_ref = refs[-3:]
    normed, _ = row_stats(x_ref[...].astype(f32))
    send_ref[...], keep_ref[...] = core_halves(normed * gain_ref[...], core_ref[0])
    rows = mix_ref.shape[0]
    width = mix_ref.shape[1] // 3
    i = pl.program_id(0)
    own = pl.ds(pl.multiple_of(i * rows, rows) + HALF, rows)
    is_first = (i == 0).astype(f32)
    is_last = (i == pl.num_programs(0) - 1).astype(f32)
    at = 0
    for n in range(len(refs) // 3 - 1):
        dq_ref, dk_ref, dv_ref = refs[3 * n : 3 * n + 3]
        part = dq_ref.shape[1]
        pad = jnp.zeros((rows - HALF, part), f32)
        cos = jnp.concatenate([cos_ref[own, :]] * (part // 128), axis=1)
        sin = jnp.concatenate([sin_ref[own, :]] * (part // 128), axis=1)

        def joined(ref, start):
            cols = slice(start, start + part)
            head = first_ref[:, cols].astype(f32) * is_first
            tail = last_ref[:, cols].astype(f32) * is_last
            ends = jnp.concatenate([head, pad], axis=0) + jnp.concatenate([pad, tail], axis=0)
            return ref[own, :].astype(f32) + ends

        mix_ref[:, at : at + part] = dq_ref[...]
        dk = joined(dk_ref, at)
        dk = (dk * cos + turn_lanes(dk * sin, 1.0)).astype(bf16)
        mix_ref[:, width + at : width + at + part] = dk
        dv = joined(dv_ref, width + at)
        mix_ref[:, 2 * width + at : 2 * width + at + part] = dv.astype(bf16)
        at += part


def mixed_call(core, x, gain, pieces, first, last, cos, sin):
    rows = x.shape[0]
    width = sum(piece[0].shape[1] for piece in pieces)
    blk = 256
    specs = []
    for dq, dk, dv in pieces:
        specs += [row_spec(blk, dq.shape[1]), const_spec(dk.shape), const_spec(dv.shape)]
    return pl.pallas_call(
        mixed_kernel,
        grid=(rows // blk,),
        in_specs=[flag_spec(), row_spec(blk, width), const_spec(gain.shape)]
        + [const_spec(y.shape) for y in (first, last, cos, sin)]
        + specs,
        out_specs=[row_spec(blk, 3 * width)] + [row_spec(blk, width // 2)] * 2,
        out_shape=[jax.ShapeDtypeStruct((rows, 3 * width), bf16)]
        + [jax.ShapeDtypeStruct((rows, width // 2), bf16)] * 2,
        compiler_params=params(32),
        cost_estimate=SMALL,
        name="mixed",
    )(core, x, gain, first, last, cos, sin, *[y for piece in pieces for y in piece])


def input_grad_kernel(mix_ref, w_ref, x_ref, gmid_ref, gain_ref, *refs):
    out_ref, gain_grad_ref = refs[-2:]
    grad_n = nn(mix_ref[...], w_ref[...])
    normed, inv = row_stats(x_ref[...].astype(f32))

    @pl.when(pl.program_id(0) == 0)
    def _():
        gain_grad_ref[...] = jnp.zeros(gain_grad_ref.shape, f32)

    gain_grad_ref[...] += fold_rows(grad_n * normed)
    u = grad_n * gain_ref[...]
    out_ref[...] = (
        gmid_ref[...]
        + inv
        * (
            u
            - jnp.mean(u, axis=-1, keepdims=True)
            - normed * jnp.mean(u * normed, axis=-1, keepdims=True)
        )
    ).astype(bf16)


def input_grad_call(mix, w, x, gmid, gain, after):
    rows, width = x.shape
    blk = 256
    return pl.pallas_call(
        input_grad_kernel,
        grid=(rows // blk,),
        in_specs=[
            row_spec(blk, 3 * width),
            const_spec(w.shape),
            row_spec(blk, width),
            row_spec(blk, width),
            const_spec((1, width)),
        ]
        + [pl.BlockSpec(memory_space=pl.ANY)] * len(after),
        out_specs=[row_spec(blk, width), pl.BlockSpec((8, width), lambda i: (0, 0))],
        out_shape=[
            jax.ShapeDtypeStruct((rows, width), bf16),
            jax.ShapeDtypeStruct((8, width), f32),
        ],
        compiler_params=params(40),
        cost_estimate=SMALL,
        name="input_grad",
    )(mix, w, x, gmid, gain, *after)


def assemble_kernel(place_ref, mine_ref, theirs_ref, in_ref, out_ref, attn_ref, qkv_ref, gain_ref):
    a = mine_ref[0].astype(f32)
    b = theirs_ref[0].astype(f32)
    cols = a.shape[1]
    first = (jnp.zeros((1, cols), jnp.int32) + place_ref[0]) == 0
    for part, at in ((jnp.where(first, a, b), 0), (jnp.where(first, b, a), cols)):
        sl = slice(at, at + cols)
        in_ref[0, 0, :, sl] = part[:72]
        in_ref[1, 0, :, sl] = part[72:144]
        out_ref[0, :, sl] = part[144:216]
        attn_ref[0, :, sl] = part[216:264]
        for c in range(3):
            qkv_ref[c, 0, :, sl] = part[264 + 48 * c : 312 + 48 * c]
        gain_ref[0, :, sl] = part[408:]


def assemble_call(place, mine, theirs):
    width = 2 * mine.shape[2]
    block = pl.BlockSpec((1,) + mine.shape[1:], lambda n, place: (n, 0, 0))
    flat = lambda n, place: (place[1] ^ n, 0, 0)
    deep = lambda n, place: (0, place[1] ^ n, 0, 0)
    shapes = [(2, 4, 72, width), (4, 72, width), (4, 48, width), (3, 4, 48, width), (4, 8, width)]
    return pl.pallas_call(
        assemble_kernel,
        grid_spec=pltpu.PrefetchScalarGridSpec(
            num_scalar_prefetch=1,
            grid=(4,),
            in_specs=[block, block],
            out_specs=[
                pl.BlockSpec((2, 1, 72, width), deep),
                pl.BlockSpec((1, 72, width), flat),
                pl.BlockSpec((1, 48, width), flat),
                pl.BlockSpec((3, 1, 48, width), deep),
                pl.BlockSpec((1, 8, width), flat),
            ],
        ),
        out_shape=[jax.ShapeDtypeStruct(shape, f32) for shape in shapes],
        compiler_params=params(32),
        cost_estimate=SMALL,
        name="assemble",
    )(place, mine, theirs)


def dp_swap(x, mask):
    count = lax.axis_size("dp")
    return lax.ppermute(x, "dp", [(i, i ^ mask) for i in range(count)])


def ring_shift(x, step):
    count = lax.axis_size("tensor")
    return lax.ppermute(x, "tensor", [(i, (i + step) % count) for i in range(count)])


def pair_swap(x):
    count = lax.axis_size("tensor")
    return lax.ppermute(x, "tensor", [(i, i ^ 1) for i in range(count)])


def index_dim(x, at, dim):
    return lax.squeeze(lax.dynamic_slice_in_dim(x, at, 1, dim), (dim,))


def core_rows(x, core, dim):
    rows = x.shape[dim]
    size = (rows // 2 + 7) // 8 * 8
    step = (rows - size) // 8
    tiles = x.reshape(x.shape[:dim] + (rows // 8, 8) + x.shape[dim + 1 :])
    part = lax.dynamic_slice_in_dim(tiles, core * step, size // 8, dim)
    return part.reshape(x.shape[:dim] + (size,) + x.shape[dim + 1 :])


def join_cores(a, b, rows, dim):
    size = a.shape[dim]
    keep = rows - size
    return jnp.concatenate([a, lax.slice_in_dim(b, size - keep, size, axis=dim)], axis=dim)


def hold(value, *after):
    return lax.optimization_barrier((value,) + after)[0]


def spread_quads(piece):
    half = (piece.shape[1] // 2 + 7) // 8 * 8
    from_x = dp_swap(piece, XBIT)
    from_y = dp_swap(piece, YBIT)
    return piece, from_x, from_y, half


def spread_diag(piece, from_x, from_y, half):
    diag_x = dp_swap(from_y[:, :half], XBIT)
    diag_y = dp_swap(from_x[:, half:], YBIT)
    early = dp_swap(jnp.stack([piece, from_x, from_y]), CORE)
    return early, diag_x, diag_y


def spread_core(piece, from_x, from_y, early, diag_x, diag_y):
    diag = jnp.concatenate([diag_x, diag_y], axis=1)
    late = dp_swap(diag, CORE)
    return [piece, from_x, from_y, diag], [early[0], early[1], early[2], late]


def spread_all(piece, *after):
    mine = jnp.stack([piece] + [dp_swap(piece, mask) for mask in (XBIT, YBIT, XBIT | YBIT)])
    theirs = dp_swap(hold(mine, *after), CORE)
    return mine, theirs


def ring_pieces(piece):
    return jnp.stack([ring_shift(piece, s) for s in range(1, lax.axis_size("tensor"))])


def by_core(mine, theirs, core):
    first = core == 0
    return jnp.where(first, mine, theirs), jnp.where(first, theirs, mine)


def add(a, b):
    return (a.astype(f32) + b.astype(f32)).astype(bf16)


def halve(arr, at, mask, dim):
    send = index_dim(arr, 1 - at, dim)
    return index_dim(arr, at, dim), dp_swap(send, mask), send


def reduce_first(total, quad):
    steps, _, rows, width = total.shape
    grid = total.reshape(steps, 2, 2, rows, width)
    half = steps // 2
    keep_x, got_x, send_x = halve(grid[:half], quad & 1, XBIT, 2)
    keep_y, got_y, send_y = halve(grid[half:], quad >> 1, YBIT, 1)
    return (keep_x, got_x, keep_y, got_y), (send_x, send_y)


def reduce_second(keep_x, got_x, keep_y, got_y, quad):
    first = add(keep_x, got_x)
    second = add(keep_y, got_y)
    keep_y, got_y, send_y = halve(first, quad >> 1, YBIT, 1)
    keep_x, got_x, send_x = halve(second, quad & 1, XBIT, 1)
    return (keep_y, got_y, keep_x, got_x), (send_y, send_x)


def reduce_ring(keep_y, got_y, keep_x, got_x, extra=None):
    first = add(keep_y, got_y)
    second = add(keep_x, got_x)
    half = first.shape[0]
    steps = half + second.shape[0]
    parts = [first[s] for s in range(half)] + [second[s] for s in range(steps - half)]
    mask = 8
    if lax.axis_size("dp") > mask:
        block = jnp.stack(parts)
        while mask < lax.axis_size("dp"):
            block = add(block, dp_swap(block, mask))
            mask *= 2
        parts = [block[s] for s in range(steps)]
    if extra is not None:
        parts = [jnp.concatenate([part, extra]) for part in parts]
    return [parts[0]] + [ring_shift(parts[s], -s) for s in range(1, steps)], parts[1:]


def reduce_sum(parts):
    result = parts[0].astype(f32)
    for part in parts[1:]:
        result = result + part.astype(f32)
    return result.astype(bf16)


def put(buf, part, starts):
    return lax.dynamic_update_slice(buf, part, starts)


def tables(seg_ids, first_row, rows):
    count = seg_ids.shape[0]
    places = jnp.arange(count, dtype=jnp.int32)
    earlier = jnp.concatenate([jnp.full((1,), -1, jnp.int32), seg_ids[:-1]])
    starts = jnp.where(seg_ids != earlier, places, 0)
    positions = places - lax.cummax(starts, axis=0)
    ext = rows + WINDOW
    seg_ext = lax.dynamic_slice(jnp.pad(seg_ids, HALF, constant_values=-1), (first_row,), (ext,))
    pos_ext = lax.dynamic_slice(jnp.pad(positions, HALF), (first_row,), (ext,))
    freq = ROPE_BASE ** (-jnp.arange(0, 64, 2).astype(f32) / 64)
    angles = pos_ext.astype(f32)[:, None] * jnp.concatenate([freq] * 4)[None, :]
    blocks = rows // BLK
    seg_rows = seg_ext.reshape(blocks + 1, BLK)
    seg_k = jnp.concatenate([seg_rows[:-1], seg_rows[1:]], axis=1)
    seg_q = seg_ext[HALF : HALF + rows].reshape(blocks, BLK)
    k_place = jnp.arange(2 * BLK, dtype=jnp.int32)[:, None] - HALF
    q_place = jnp.arange(BLK, dtype=jnp.int32)[None, :]
    near = jnp.abs(k_place - q_place) <= HALF
    allowed = near[None] & (seg_k[:, :, None] == seg_q[:, None, :])
    bias = jnp.where(allowed, 0.0, -1e30).astype(f32)
    return jnp.cos(angles), jnp.sin(angles), bias, pos_ext


def body(
    hidden_in,
    seg_ids,
    norm1_gain,
    norm2_gain,
    qkv_weight,
    attn_weight,
    mlp_in_weight,
    mlp_out_weight,
    out_grad,
):
    rows, width = hidden_in.shape
    steps = lax.axis_size("tensor")
    here = lax.axis_index("tensor")
    at_dp = lax.axis_index("dp")
    core = at_dp & 1
    quad = (at_dp >> 1) & 3
    odd = (here & 1) == 1
    w_qkv = qkv_weight.transpose(1, 2, 3, 0).reshape(3, 4, 48, width)
    w_in = mlp_in_weight.transpose(1, 2, 0).reshape(2, 4, 72, width)
    w_out = mlp_out_weight.reshape(4, 72, width)
    w_attn = attn_weight.reshape(4, 48, width)

    own_qkv = core_rows(index_dim(w_qkv, quad, 1), core, 1).reshape(3 * 24, width)
    ring_qkv = ring_pieces(own_qkv)
    x_held = hold(hidden_in, ring_qkv)
    edge = jnp.where(odd, x_held[:HALF], x_held[-HALF:])
    halo = pair_swap(edge)
    none = jnp.zeros_like(halo)
    x_ext = jnp.concatenate(
        [jnp.where(odd, halo, none), x_held, jnp.where(odd, none, halo)], axis=0
    )

    cos, sin, bias, pos_ext = tables(hold(seg_ids, ring_qkv), here * rows, rows)
    quads_qkv = spread_quads(ring_qkv)
    diag_qkv = spread_diag(*quads_qkv)
    wi_held = hold(w_in, pos_ext)
    wo_held = hold(w_out, pos_ext)
    wa_held = hold(w_attn, pos_ext)
    own_rest = jnp.concatenate(
        [
            index_dim(index_dim(wi_held, core, 0), quad, 0),
            core_rows(index_dim(wo_held, quad, 0), core, 0),
            core_rows(index_dim(wa_held, quad, 0), core, 0),
        ],
        axis=0,
    )
    ring_rest = ring_pieces(own_rest)
    quads_rest = spread_quads(ring_rest)
    mine, theirs = spread_core(*quads_qkv[:3], *diag_qkv)
    qkv_all = jnp.zeros((3, steps, 4, 48, width), bf16)
    qkv_all = qkv_all.at[:, 0].set(hold(w_qkv, quads_qkv[1], quads_qkv[2]))
    for n in range(4):
        a, b = by_core(mine[n], theirs[n], core)
        a = a.reshape(steps - 1, 3, 24, width)
        b = b.reshape(steps - 1, 3, 24, width)
        part = join_cores(a, b, 48, 2).transpose(1, 0, 2, 3)[:, :, None]
        qkv_all = put(qkv_all, part, (0, 1, quad ^ n, 0, 0))
    qkv_all = qkv_all.reshape(3, width, width)

    gain_one = norm1_gain[None]
    gain_two = norm2_gain[None]
    q, k, v = qkv_call(x_ext, gain_one, hold(qkv_all, ring_rest), cos, sin)
    low_attn, lse = attend_call(q, k, v, bias, rows)

    piece, from_x, from_y, half = quads_rest
    early, diag_x, diag_y = spread_diag(piece, hold(from_x, q), hold(from_y, q), half)
    mine, theirs = spread_core(piece, from_x, from_y, early, hold(diag_x, low_attn), diag_y)
    wi_held = hold(w_in, q)
    wo_held = hold(w_out, q)
    wa_held = hold(w_attn, q)
    in_all = jnp.zeros((2, steps, 4, 72, width), bf16).at[:, 0].set(wi_held)
    out_all = jnp.zeros((steps, 4, 72, width), bf16).at[0].set(wo_held)
    attn_all = jnp.zeros((steps, 4, 48, width), bf16).at[0].set(wa_held)
    for n in range(4):
        a, b = by_core(mine[n], theirs[n], core)
        pair = jnp.stack([a[:, :72], b[:, :72]])[:, :, None]
        in_all = put(in_all, pair, (0, 1, quad ^ n, 0, 0))
        out_all = put(
            out_all, join_cores(a[:, 72:112], b[:, 72:112], 72, 1)[:, None], (1, quad ^ n, 0, 0)
        )
        attn_all = put(
            attn_all, join_cores(a[:, 112:], b[:, 112:], 48, 1)[:, None], (1, quad ^ n, 0, 0)
        )
    ff = steps * 288
    in_all = in_all.reshape(2, ff, width)
    out_all = out_all.reshape(ff, width)
    attn_all = attn_all.reshape(width, width)

    core_flag = core.astype(jnp.int32)[None]
    (
        result,
        grad_mid,
        dattn,
        mid_send,
        mid_keep,
        two_send,
        two_keep,
        og_send,
        og_keep,
        low_act,
        ggu,
        gain_two_part,
    ) = mlp_call(
        core_flag, hidden_in, out_grad, low_attn, gain_two, attn_all, in_all, out_all
    )

    def grads(x, ys, *lead):
        shape = lead + (steps, 4, x.shape[1] // (4 * steps * lead[0] if lead else 4 * steps))
        return [tn(x, y).astype(bf16).reshape(shape + (width // 2,)) for y in ys]

    g_in = grads(ggu, (two_send, two_keep), 2)
    g_out = grads(low_act, (og_send, og_keep))
    g_attn = grads(low_attn, (mid_send, mid_keep))
    got_in = dp_swap(g_in[0], CORE)
    got_out = dp_swap(g_out[0], CORE)
    got_attn = dp_swap(g_attn[0], CORE)
    dattn = hold(dattn, *g_in, *g_out, *g_attn)
    piece_a = attend_back_call(q, k, v, dattn, bias, lse, cos, sin, 3, 128)
    sum_in = add(g_in[1], hold(got_in, piece_a[0]))
    core_rest = jnp.concatenate(
        [sum_in[0], sum_in[1], add(g_out[1], got_out), add(g_attn[1], got_attn)], axis=2
    )
    first_rest, _ = reduce_first(core_rest, quad)
    dattn = hold(dattn, core_rest, piece_a[0])
    piece_b = attend_back_call(q, k, v, dattn, bias, lse, cos, sin, 0, 384)
    dattn = hold(dattn, *first_rest[1::2], piece_b[0])
    piece_c = attend_back_call(q, k, v, dattn, bias, lse, cos, sin, 2, 256)
    second_rest, _ = reduce_second(*first_rest, quad)
    pieces = (piece_b, piece_a, piece_c)
    ends = [
        jnp.concatenate([jnp.where(odd, x[:HALF], x[-HALF:]) for x in (p[n] for p in pieces)], axis=1)
        for n in (1, 2)
    ]
    got = pair_swap(jnp.stack(ends, axis=1))
    turn = width // steps
    got = jnp.where(odd, jnp.roll(got, turn, 2), jnp.roll(got, -turn, 2)).reshape(HALF, 2 * width)
    none = jnp.zeros_like(got)
    own = slice(HALF, HALF + rows)
    mix, one_send, one_keep = mixed_call(
        core_flag,
        hidden_in,
        gain_one,
        pieces,
        jnp.where(odd, got, none),
        jnp.where(odd, none, got),
        cos,
        sin,
    )
    g_qkv = [
        tn(mix, y).astype(bf16).reshape(3, steps, 4, 48, width // 2)
        for y in (one_send, one_keep)
    ]
    got_qkv = dp_swap(g_qkv[0], CORE)
    core_qkv = add(g_qkv[1], got_qkv).transpose(1, 2, 0, 3, 4).reshape(steps, 4, 144, width // 2)
    first_qkv, sent_qkv = reduce_first(core_qkv, quad)
    ring_back, sent_rest = reduce_ring(*second_rest)
    grad_hidden, gain_one_part = input_grad_call(
        mix,
        qkv_all.reshape(3 * width, width),
        hidden_in,
        grad_mid,
        gain_one,
        (*sent_qkv, *sent_rest),
    )
    gains = jnp.stack([jnp.sum(gain_one_part, axis=0), jnp.sum(gain_two_part, axis=0)])
    mask = 8
    while mask < lax.axis_size("dp"):
        gains = gains + dp_swap(gains, mask)
        mask *= 2

    def coded(x):
        high = lax.reduce_precision(x, 8, 7)
        return jnp.concatenate([high, x - high]).astype(bf16).reshape(8, width // 2)

    def decoded(x):
        both = x.astype(f32).reshape(x.shape[:-2] + (2, 2, width))
        return both[..., 0, :, :] + both[..., 1, :, :]

    second_qkv, _ = reduce_second(*first_qkv, quad)
    parts, _ = reduce_ring(*second_qkv, coded(gains))
    slots = jnp.zeros((steps, 8, width // 2), bf16)
    for s in range(steps):
        slots = put(slots, parts[s][None, 144:], ((here + s) % steps if s else here, 0, 0))
    gains = jnp.sum(decoded(slots), axis=0)
    rest = reduce_sum(ring_back)
    qkv_total = reduce_sum([part[:144] for part in parts])

    mine, theirs = spread_all(jnp.concatenate([rest, qkv_total, coded(gains)]))
    place = jnp.stack([core, quad]).astype(jnp.int32)
    o_in, o_out, o_attn, o_qkv, slots = assemble_call(place, mine, theirs)
    slots = slots.reshape(4, 8, 2, width // 2).transpose(0, 2, 1, 3)
    gains = jnp.sum(decoded(slots.reshape(8, 8, width // 2)), axis=0)
    grad_qkv = o_qkv.reshape(3, 3, 64, width).transpose(3, 0, 1, 2)
    grad_in = o_in.reshape(2, 288, width).transpose(2, 0, 1)
    return (
        result,
        grad_hidden,
        gains[0],
        gains[1],
        grad_qkv,
        o_attn.reshape(192, width),
        grad_in,
        o_out.reshape(288, width),
    )


def solution(mesh):
    rows = P(("dp", "tensor"), None)
    in_specs = (
        rows,
        P("dp"),
        P(),
        P(),
        P(None, None, "tensor", None),
        P("tensor", None),
        P(None, None, "tensor"),
        P("tensor", None),
        rows,
    )
    out_specs = (
        rows,
        rows,
        P(),
        P(),
        P(None, None, "tensor", None),
        P("tensor", None),
        P(None, None, "tensor"),
        P("tensor", None),
    )
    return jax.shard_map(body, mesh=mesh, in_specs=in_specs, out_specs=out_specs, check_vma=False)
```
